256 devices in a mesh: dp: 4 (over z_hi, core), mp: 64 (over y, z_lo, x).
Axes of the slice: x: 4, y: 4, z: 8 (z_hi: 2, z_lo: 4; z = z_hi * 4 + z_lo), core: 2. Of those that a mesh axis runs over, the one named last changes fastest.
Arguments:
- tokens: bfloat16 [1024, 6144], P(('dp', 'mp')), may hold values from -6 to 6
- cotangent: bfloat16 [1024, 6144], P(('dp', 'mp')), may hold values from -6 to 6
- ln_gain: float32 [6144], replicated, may hold values from 0.5 to 1.5
- qk_gain: float32 [2, 128], replicated, may hold values from 0.5 to 6
- w_qkv: bfloat16 [3, 4096, 6144], P(None, 'mp'), may hold values from -0.05103104 to 0.05103104
- w_mlp_in: bfloat16 [16384, 6144], P('mp'), may hold values from -0.078125 to 0.078125
- w_attn_out: bfloat16 [4096, 6144], P('mp'), may hold values from -0.0390625 to 0.0390625
- w_mlp_out: bfloat16 [16384, 6144], P('mp'), may hold values from -0.0390625 to 0.0390625
Outputs:
- output: bfloat16 [1024, 6144], P(('dp', 'mp'))
- d_tokens: bfloat16 [1024, 6144], P(('dp', 'mp'))
- g_ln_gain: float32 [6144], replicated
- g_qk_gain: float32 [2, 128], replicated
- g_w_qkv: bfloat16 [3, 4096, 6144], P(None, 'mp', 'dp')
- g_w_mlp_in: bfloat16 [16384, 6144], P('mp', 'dp')
- g_w_attn_out: bfloat16 [4096, 6144], P('mp', 'dp')
- g_w_mlp_out: bfloat16 [16384, 6144], P('mp', 'dp')
The draws below stay inside these ranges and needn't reach their ends.
All inputs are finite; a program needn't handle non-finite values.
Results may differ from the reference program's by a relative error of at most 0.034.
The reference program's roundings to bfloat16 on the way count: a program that leaves them out, or rounds other values in their place, can miss the bound.
Values may be sent and summed in bfloat16 or wider, within the bound.
No kernel may reach another device: no remote copies, remote signals or barrier semaphores. Data moves between devices by JAX's collectives and lax.ppermute only.
A program may use at most 128 MiB of HBM per device.

```python
import math
import jax
import jax.numpy as jnp
from jax import lax

D = 6144
HD = 128
HEADS = 32
FF = 16384
PATCHES = 256
IMAGES = 4
TOKENS = 1024
HA = 4096
N_DP = 4


def draw_qk_gain(key, part):
    key = jax.random.fold_in(key, 5)
    gains_drawn = jax.random.uniform(key, (2, HD), jnp.float32, 0.5, 2.0)
    return gains_drawn


def draw_w_qkv(key, part):
    key = jax.random.fold_in(key, 11)
    first_key = jax.random.fold_in(key, 0)
    scale_in = 1.0 / jnp.sqrt(jnp.float32(D))
    weights_drawn = jax.random.normal(first_key, (3, HA, D), jnp.float32) * scale_in
    limit = 4.0 * scale_in
    return jnp.clip(weights_drawn, -limit, limit).astype(jnp.bfloat16)


def block_scale(own_key, dims, cuts, low, high):
    gain = 1.0
    for axis_at, parts in cuts:
        heights = jax.random.uniform(jax.random.fold_in(jax.random.fold_in(own_key, 6), axis_at), (parts,), jnp.float32, low / len(cuts), high / len(cuts))
        gain = gain * jnp.repeat(jnp.exp(heights), dims[axis_at] // parts).reshape((-1,) + (1,) * (len(dims) - 1 - axis_at))
    return gain


def noise(stream_key, extent, spread, most, cuts=(), held_as=jnp.bfloat16):
    values = spread * jax.random.normal(stream_key, extent, jnp.float32)
    if cuts:
        values = values * block_scale(stream_key, extent, cuts, -0.22, 0.18)
    return jnp.clip(values, -most, most).astype(held_as)


def setup_inputs(seed: int = 0) -> dict:
    arg_keys = jax.random.split(jax.random.key(seed), 9)
    return {
        "tokens": noise(arg_keys[0], (TOKENS, D), 1.0, 6.0, ((0, 256),)),
        "cotangent": noise(arg_keys[1], (TOKENS, D), 1.0, 6.0, ((0, 256),)),
        "ln_gain": jnp.clip(1.0 + 0.1 * jax.random.normal(arg_keys[2], (D,), jnp.float32), 0.5, 1.5),
        "qk_gain": draw_qk_gain(jax.random.fold_in(arg_keys[8], 71), 0),
        "w_qkv": draw_w_qkv(jax.random.fold_in(arg_keys[8], 71), 0),
        "w_mlp_in": noise(arg_keys[5], (FF, D), D ** -0.5, 0.078125, ((0, 64),)),
        "w_attn_out": noise(arg_keys[6], (HA, D), (HA + FF) ** -0.5, 0.0390625, ((0, 64),)),
        "w_mlp_out": noise(arg_keys[7], (FF, D), (HA + FF) ** -0.5, 0.0390625, ((0, 64),)),
    }


EPS = 1e-06

def standardize(values):
    average = lax.optimization_barrier(jnp.mean(values, -1, keepdims=True))
    centered = values - average
    inv_std = lax.rsqrt(lax.optimization_barrier(jnp.mean(centered * centered, -1, keepdims=True)) + EPS)
    return (centered * inv_std, inv_std)

def norm_back(gradient, scaled, inv_std, gain_row):
    weighted = gradient * gain_row
    return inv_std * (weighted - lax.optimization_barrier(jnp.mean(weighted, -1, keepdims=True)) - scaled * lax.optimization_barrier(jnp.mean(weighted * scaled, -1, keepdims=True)))

def gelu_slope(hidden_pre):
    normal_cdf = 0.5 * (1.0 + lax.erf(hidden_pre * 0.7071067811865476))
    normal_pdf = jnp.exp(-0.5 * hidden_pre * hidden_pre) * 0.3989422804014327
    return normal_cdf + hidden_pre * normal_pdf

def times_rows(left, weight):
    return lax.dot_general(left, weight, (((1,), (1,)), ((), ())), preferred_element_type=jnp.float32)

def row_contract(left, right):
    return lax.dot_general(left, right, (((0,), (0,)), ((), ())), preferred_element_type=jnp.float32)

def image_attention(inputs, qk_gain):
    query, key_raw, values_bf, d_context = inputs
    q_scaled, q_inv = standardize(query)
    k_scaled, k_inv = standardize(key_raw)
    q_normed = (q_scaled * qk_gain[0]).astype(jnp.bfloat16)
    k_normed = (k_scaled * qk_gain[1]).astype(jnp.bfloat16)
    scores = jnp.einsum('qhd,khd->hqk', q_normed.astype(jnp.float32), k_normed.astype(jnp.float32)) / math.sqrt(HD)
    attn_probs = jax.nn.softmax(scores, -1).astype(jnp.bfloat16)
    probs_f = attn_probs.astype(jnp.float32)
    values_f = values_bf.astype(jnp.float32)
    context = jnp.einsum('hqk,khd->qhd', probs_f, values_f).astype(jnp.bfloat16)
    d_ctx_f = d_context.astype(jnp.float32)
    d_probs = jnp.einsum('qhd,khd->hqk', d_ctx_f, values_f)
    d_scores = (probs_f * (d_probs - lax.optimization_barrier(jnp.sum(probs_f * d_probs, -1, keepdims=True))) / math.sqrt(HD)).astype(jnp.bfloat16)
    d_values = jnp.einsum('hqk,qhd->khd', probs_f, d_ctx_f)
    d_qn = jnp.einsum('hqk,khd->qhd', d_scores.astype(jnp.float32), k_normed.astype(jnp.float32))
    d_kn = jnp.einsum('hqk,qhd->khd', d_scores.astype(jnp.float32), q_normed.astype(jnp.float32))
    d_query = norm_back(d_qn, q_scaled, q_inv, qk_gain[0])
    d_key = norm_back(d_kn, k_scaled, k_inv, qk_gain[1])
    gain_terms = jnp.stack([lax.optimization_barrier(jnp.sum(d_qn * q_scaled, (0, 1))), lax.optimization_barrier(jnp.sum(d_kn * k_scaled, (0, 1)))])
    return (context, d_query, d_key, d_values, gain_terms)

def reference(tokens, cotangent, ln_gain, qk_gain, w_qkv, w_mlp_in, w_attn_out, w_mlp_out):
    x_float = tokens.astype(jnp.float32)
    scaled_in, inv_std = standardize(x_float)
    normed = (scaled_in * ln_gain).astype(jnp.bfloat16)
    w_flat = w_qkv.reshape(3 * HA, D)
    projected = times_rows(normed, w_flat).reshape(TOKENS, 3, HA)
    hidden_pre = times_rows(normed, w_mlp_in)
    activated = jax.nn.gelu(hidden_pre, approximate=False).astype(jnp.bfloat16)
    d_context = times_rows(cotangent, w_attn_out).astype(jnp.bfloat16)
    d_active = times_rows(cotangent, w_mlp_out).astype(jnp.bfloat16)
    shaped = (IMAGES, PATCHES, HEADS, HD)
    inputs = (projected[:, 0].reshape(shaped), projected[:, 1].reshape(shaped), projected[:, 2].astype(jnp.bfloat16).reshape(shaped), d_context.reshape(shaped))
    context, d_query, d_key, d_values, gain_terms = lax.map(lambda pieces: image_attention(pieces, qk_gain), inputs)
    context = context.reshape(TOKENS, HA)
    mixed_sum = x_float + jnp.dot(context, w_attn_out, preferred_element_type=jnp.float32) + jnp.dot(activated, w_mlp_out, preferred_element_type=jnp.float32)
    output = mixed_sum.astype(jnp.bfloat16)
    d_in = jnp.stack([d_query.reshape(TOKENS, HA), d_key.reshape(TOKENS, HA), d_values.reshape(TOKENS, HA)], 1).astype(jnp.bfloat16)
    d_in_flat = d_in.reshape(TOKENS, 3 * HA)
    d_hidden = (d_active.astype(jnp.float32) * gelu_slope(hidden_pre)).astype(jnp.bfloat16)
    d_normed = jnp.dot(d_in_flat, w_flat, preferred_element_type=jnp.float32) + jnp.dot(d_hidden, w_mlp_in, preferred_element_type=jnp.float32)
    d_tokens = (cotangent.astype(jnp.float32) + norm_back(d_normed, scaled_in, inv_std, ln_gain)).astype(jnp.bfloat16)
    g_ln_gain = lax.optimization_barrier(jnp.sum(d_normed * scaled_in, 0))
    g_qk_gain = lax.optimization_barrier(jnp.sum(gain_terms, 0))
    group_len = TOKENS // N_DP

    def add_group(partials, group_index):
        row_start = (group_index * group_len).astype(jnp.int32)
        norm_rows = lax.dynamic_slice_in_dim(normed, row_start, group_len, 0)
        din_rows = lax.dynamic_slice_in_dim(d_in_flat, row_start, group_len, 0)
        dhid_rows = lax.dynamic_slice_in_dim(d_hidden, row_start, group_len, 0)
        ctx_rows = lax.dynamic_slice_in_dim(context, row_start, group_len, 0)
        act_rows = lax.dynamic_slice_in_dim(activated, row_start, group_len, 0)
        cot_rows = lax.dynamic_slice_in_dim(cotangent, row_start, group_len, 0)
        terms = (row_contract(din_rows, norm_rows), row_contract(dhid_rows, norm_rows), row_contract(ctx_rows, cot_rows), row_contract(act_rows, cot_rows))
        rounded = tuple((lax.optimization_barrier(term.astype(jnp.bfloat16)).astype(jnp.float32) for term in terms))
        return (tuple((total + term for total, term in zip(partials, rounded))), None)
    initial = (jnp.zeros((3 * HA, D), jnp.float32), jnp.zeros((FF, D), jnp.float32), jnp.zeros((HA, D), jnp.float32), jnp.zeros((FF, D), jnp.float32))
    sums, unused = lax.scan(add_group, initial, jnp.arange(N_DP, dtype=jnp.int32))
    g_w_qkv = sums[0].reshape(3, HA, D).astype(jnp.bfloat16)
    return (output, d_tokens, g_ln_gain, g_qk_gain, g_w_qkv, sums[1].astype(jnp.bfloat16), sums[2].astype(jnp.bfloat16), sums[3].astype(jnp.bfloat16))
```

```python
import functools
import math

import jax
import jax.numpy as jnp
from jax import lax
from jax.experimental import pallas as pl
from jax.experimental.pallas import tpu as pltpu
from jax.sharding import PartitionSpec as P

D = 6144
HD = 128
ROWS = 256
QUARTER = D // 4
EPS = 1e-06
X, Z, Y = 1, 4, 16
BF16 = jnp.bfloat16
F32 = jnp.float32
VMEM = pl.BlockSpec(memory_space=pltpu.VMEM)
SMEM = pl.BlockSpec(memory_space=pltpu.SMEM)
ANY = pl.BlockSpec(memory_space=pl.ANY)
PARAMS = pltpu.CompilerParams(vmem_limit_bytes=48 * 1024 * 1024)


def shape(*dims, dtype=BF16):
    return jax.ShapeDtypeStruct(dims, dtype)


def swapped(block, axis, mask):
    count = lax.axis_size(axis)
    return lax.ppermute(block, axis, [(low, low ^ mask) for low in range(count)])


def pieces(block, unit):
    return [block] + [swapped(block, "mp", step * unit) for step in (1, 2, 3)]


def exchanged(blocks, unit):
    return [blocks[0]] + [swapped(blocks[step], "mp", step * unit) for step in (1, 2, 3)]


def two_steps(block):
    half = block.shape[1] // 2
    opposite = swapped(block, "mp", 2 * X)
    pair = jnp.concatenate([block, opposite], 0)
    return [
        block,
        opposite,
        swapped(pair[:, :half], "mp", X),
        swapped(pair[:, half:], "mp", 3 * X),
    ]


def total(blocks):
    first, second, third, fourth = (block.astype(F32) for block in blocks)
    return (first + second) + (third + fourth)


def two_parts(values):
    high = values.astype(BF16)
    return high, (values - high.astype(F32)).astype(BF16)


def standardize(values):
    average = jnp.mean(values, -1, keepdims=True)
    centered = values - average
    inv_std = lax.rsqrt(jnp.mean(centered * centered, -1, keepdims=True) + EPS)
    return (centered * inv_std, inv_std)


def norm_back(gradient, scaled, inv_std, gain_row):
    weighted = gradient * gain_row
    return inv_std * (
        weighted
        - jnp.mean(weighted, -1, keepdims=True)
        - scaled * jnp.mean(weighted * scaled, -1, keepdims=True)
    )


def times_rows(left, weight):
    return lax.dot_general(left, weight, (((1,), (1,)), ((), ())), preferred_element_type=F32)


def row_contract(left, right):
    return lax.dot_general(left, right, (((0,), (0,)), ((), ())), preferred_element_type=F32)


def dot(left, right):
    return jnp.dot(left, right, preferred_element_type=F32)


def start_kernel(tokens, cotangent, gain, out):
    scaled, _ = standardize(tokens[...].astype(F32))
    both = jnp.concatenate([scaled * gain[...], cotangent[...].astype(F32)], 0)
    out[...] = both.astype(BF16)


def start(tokens, cotangent, gain):
    return pl.pallas_call(
        start_kernel, out_shape=shape(8, D), in_specs=[VMEM] * 3, out_specs=VMEM
    )(tokens, cotangent, gain)


def apart_kernel(*refs):
    blocks = [ref[...].astype(F32) for ref in refs[:4]]
    refs[4][...] = jnp.concatenate([block[:4] for block in blocks], 0).astype(BF16)
    refs[5][...] = jnp.concatenate([block[4:] for block in blocks], 0).astype(BF16)


def apart(parts):
    return pl.pallas_call(
        apart_kernel, out_shape=[shape(16, D)] * 2, in_specs=[VMEM] * 4, out_specs=[VMEM] * 2
    )(*parts)


def join_kernel(place, *refs):
    n_out, c_out, away = refs[8:]
    left = pl.multiple_of((1 - place[0]) * (D // 2), D // 2)
    for at in range(4):
        rows = slice(16 * at, 16 * at + 16)
        n_out[rows, :] = refs[at][...]
        c_out[rows, :] = refs[4 + at][...]
        away[rows, :] = refs[at][:, pl.ds(left, D // 2)]
        away[64 + 16 * at : 80 + 16 * at, :] = refs[4 + at][:, pl.ds(left, D // 2)]


def join(place, n_parts, c_parts):
    return pl.pallas_call(
        join_kernel,
        out_shape=[shape(64, D), shape(64, D), shape(128, D // 2)],
        in_specs=[SMEM] + [VMEM] * 8,
        out_specs=[VMEM] * 3,
    )(place, *n_parts, *c_parts)


def n_moves(parts, target):
    return [(parts[at], target.at[pl.ds(64 * at, 64)]) for at in range(4)]


def c_moves(parts, target):
    half = parts[0].shape[1] // 2
    left, right = pl.ds(0, half), pl.ds(half, half)
    moves = []
    for up in range(4):
        rows = pl.ds(16 * up, 16)
        lower = pl.ds(64 + 16 * up, 16)
        spots = [pl.ds(64 * up + 16 * at, 16) for at in range(4)]
        moves += [
            (parts[0].at[rows], target.at[spots[0]]),
            (parts[1].at[rows], target.at[spots[2]]),
            (parts[2].at[rows], target.at[spots[1], left]),
            (parts[2].at[lower], target.at[spots[3], left]),
            (parts[3].at[rows], target.at[spots[3], right]),
            (parts[3].at[lower], target.at[spots[1], right]),
        ]
    return moves


def first_kernel(*refs):
    n_parts, c_parts, weights = refs[:4], refs[4:8], refs[8:10]
    n_out, c_out, qk_ref, vd_ref = refs[10:14]
    n_all, c_all, wq, wo, sems = refs[14:]
    copies = []

    def begin(source, target):
        copy = pltpu.make_async_copy(source, target, sems.at[len(copies)])
        copy.start()
        copies.append(copy)
        return copy

    n_in = [begin(*move) for move in n_moves(n_parts, n_all)]
    wq_in = begin(weights[0], wq)
    c_in = [begin(*move) for move in c_moves(c_parts, c_all)]
    wo_in = begin(weights[1], wo)
    for copy in n_in:
        copy.wait()
    wq_in.wait()
    n_done = begin(n_all, n_out)
    cols = wo.shape[0]
    projected = jnp.zeros((ROWS, 3 * cols), F32)
    for at in range(4):
        span = slice(QUARTER * at, QUARTER * at + QUARTER)
        projected += times_rows(n_all[:, span], wq[:, span])
    qk_ref[...] = projected[:, : 2 * cols]
    for copy in c_in:
        copy.wait()
    wo_in.wait()
    c_done = begin(c_all, c_out)
    d_context = jnp.zeros((ROWS, cols), F32)
    for at in range(4):
        span = slice(QUARTER * at, QUARTER * at + QUARTER)
        d_context += times_rows(c_all[:, span], wo[:, span])
    vd_ref[...] = jnp.concatenate([projected[:, 2 * cols :], d_context], 1).astype(BF16)
    n_done.wait()
    c_done.wait()


def first(n_parts, c_parts, w_flat, w_out):
    cols = w_out.shape[0]
    return pl.pallas_call(
        first_kernel,
        out_shape=[
            shape(ROWS, D),
            shape(ROWS, D),
            shape(ROWS, 2 * cols, dtype=F32),
            shape(ROWS, 2 * cols),
        ],
        in_specs=[ANY] * 10,
        out_specs=[ANY, ANY, VMEM, VMEM],
        scratch_shapes=[
            pltpu.VMEM((ROWS, D), BF16),
            pltpu.VMEM((ROWS, D), BF16),
            pltpu.VMEM((3 * cols, D), BF16),
            pltpu.VMEM((cols, D), BF16),
            pltpu.SemaphoreType.DMA((32,)),
        ],
        compiler_params=PARAMS,
    )(*n_parts, *c_parts, w_flat, w_out)


def hidden_kernel(n_ref, c_ref, win, wout, out, *scratch):
    n_all, c_all, w_in, w_out, sems = scratch
    loads = []
    for at in range(4):
        span = pl.ds(QUARTER * at, QUARTER)
        pairs = ((n_ref, n_all), (win, w_in), (c_ref, c_all), (wout, w_out))
        for which, (source, target) in enumerate(pairs):
            copy = pltpu.make_async_copy(
                source.at[:, span], target.at[:, span], sems.at[at, which]
            )
            copy.start()
            loads.append(copy)
    units = w_in.shape[0]
    hidden = jnp.zeros((ROWS, units), F32)
    d_act = jnp.zeros((ROWS, units), F32)
    for at in range(4):
        for copy in loads[4 * at : 4 * at + 4]:
            copy.wait()
        span = slice(QUARTER * at, QUARTER * at + QUARTER)
        hidden += times_rows(n_all[:, span], w_in[:, span])
        d_act += times_rows(c_all[:, span], w_out[:, span])
    cdf = 0.5 * (1.0 + lax.erf(hidden * 0.7071067811865476))
    pdf = jnp.exp(-0.5 * hidden * hidden) * 0.3989422804014327
    out[:, units:] = (hidden * cdf).astype(BF16)
    out[:, :units] = (d_act.astype(BF16).astype(F32) * (cdf + hidden * pdf)).astype(BF16)


def hidden(n_all, c_all, w_in, w_out):
    units = w_in.shape[0]
    return pl.pallas_call(
        hidden_kernel,
        out_shape=shape(ROWS, 2 * units),
        in_specs=[ANY] * 4,
        out_specs=VMEM,
        scratch_shapes=[
            pltpu.VMEM((ROWS, D), BF16),
            pltpu.VMEM((ROWS, D), BF16),
            pltpu.VMEM((units, D), BF16),
            pltpu.VMEM((units, D), BF16),
            pltpu.SemaphoreType.DMA((4, 4)),
        ],
        compiler_params=PARAMS,
    )(n_all, c_all, w_in, w_out)


def head_kernel(place, qk_own, qk_peer, vd_own, vd_peer, gains, out, gain_ref):
    cols = HD // 2

    def whole(own, peer, left):
        other = jnp.concatenate(
            [peer[16 * (at ^ 1) : 16 * (at ^ 1) + 16, :] for at in range(ROWS // 16)], 0
        )
        return jnp.concatenate(
            [own[:, left : left + cols], other[:, left : left + cols]], 1
        )

    query, key = whole(qk_own, qk_peer, 0), whole(qk_own, qk_peer, cols)
    values, d_ctx = whole(vd_own, vd_peer, 0), whole(vd_own, vd_peer, cols)
    q_gain, k_gain = gains[0:1, :], gains[1:2, :]
    q_scaled, q_inv = standardize(query)
    k_scaled, k_inv = standardize(key)
    q_normed = (q_scaled * q_gain).astype(BF16)
    k_normed = (k_scaled * k_gain).astype(BF16)
    scores = times_rows(q_normed, k_normed) * (1.0 / math.sqrt(HD))
    grown = jnp.exp(scores - jnp.max(scores, -1, keepdims=True))
    probs = (grown / jnp.sum(grown, -1, keepdims=True)).astype(BF16)
    context = dot(probs, values)[:, :cols]
    d_probs = times_rows(d_ctx, values)
    probs_f = probs.astype(F32)
    centered = d_probs - jnp.sum(probs_f * d_probs, -1, keepdims=True)
    d_scores = (probs_f * centered * (1.0 / math.sqrt(HD))).astype(BF16)
    d_values = row_contract(probs, d_ctx)
    d_qn = dot(d_scores, k_normed)
    d_kn = row_contract(d_scores, q_normed)
    d_query = norm_back(d_qn, q_scaled, q_inv, q_gain)
    d_key = norm_back(d_kn, k_scaled, k_inv, k_gain)
    out[:, :HD] = jnp.concatenate([d_query[:, :cols], d_key[:, :cols]], 1).astype(BF16)
    out[:, HD:] = jnp.concatenate([d_values[:, :cols], context], 1).astype(BF16)
    for row, terms in enumerate((d_qn * q_scaled, d_kn * k_scaled)):
        mine = jnp.sum(terms, 0, keepdims=True)[:, :cols]
        none = jnp.zeros_like(mine)
        even = jnp.concatenate([mine, none], 1)
        odd = jnp.concatenate([none, mine], 1)
        gain_ref[row : row + 1, :] = jnp.where(place[2] == 0, even, odd)


def head(place, qk_own, qk_peer, vd_own, vd_peer, gains):
    return pl.pallas_call(
        head_kernel,
        out_shape=[shape(ROWS, 2 * HD), shape(2, HD, dtype=F32)],
        in_specs=[SMEM] + [VMEM] * 5,
        out_specs=[VMEM] * 2,
        compiler_params=PARAMS,
    )(place, qk_own, qk_peer, vd_own, vd_peer, gains)


SLAB = 640
WIDE = D + 2 * 128
STEPS = WIDE // SLAB


def back_kernel(dc, ad, w_ao, w_mo, w_qkv, w_mi, n_ref, gain, gain_part, *refs):
    outs, sums = refs[:8], refs[8]
    mix_outs, kept, opposite, near_left, near_right = outs[:4], *outs[4:]
    at = pl.program_id(0)
    ins, units = w_qkv.shape[0], w_mi.shape[0]
    mixed = dot(dc[:, ins:], w_ao[...]) + dot(ad[:, units:], w_mo[...])
    for k in range(4):
        mix_outs[k][...] = mixed[64 * k : 64 * k + 64].astype(BF16)
    d_norm = dot(dc[:, :ins], w_qkv[...]) + dot(ad[:, :units], w_mi[...])
    part = jnp.sum(d_norm * n_ref[...].astype(F32), 0, keepdims=True) / gain[...]

    @pl.when(at == 0)
    def _():
        sums[48:64, :] = jnp.zeros((16, 128), F32)
        sums[48:50, :] = gain_part[...]

    for k in range(3):
        sums[pl.ds(5 * at + k, 1), :] = part[:, 128 * k : 128 * k + 128]

    @pl.when(at < STEPS - 1)
    def _():
        for k in (3, 4):
            sums[pl.ds(5 * at + k, 1), :] = part[:, 128 * k : 128 * k + 128]

    chunks = [
        jnp.concatenate(
            [d_norm[64 * up + 16 * k : 64 * up + 16 * k + 16] for up in range(4)], 0
        ).astype(BF16)
        for k in range(4)
    ]
    kept[...] = chunks[0]
    opposite[...] = chunks[2]

    @pl.when(at < STEPS // 2)
    def _():
        near_left[:64, :] = chunks[1]
        near_left[64:, :] = chunks[3]

    @pl.when(at >= STEPS // 2)
    def _():
        near_right[:64, :] = chunks[3]
        near_right[64:, :] = chunks[1]

    @pl.when(at == STEPS - 1)
    def _():
        high, low = two_parts(sums[...])
        for out, rows in ((kept, 0), (opposite, 0), (near_right, 0), (near_right, 64)):
            out[rows : rows + 64, SLAB - 256 : SLAB - 128] = high
            out[rows : rows + 64, SLAB - 128 :] = low


def back(dc, ad, w_ao, w_mo, w_qkv, w_mi, n_all, ln_gain, gain_part):
    smalls, larges = (dc, ad), (w_ao, w_mo, w_qkv, w_mi, n_all, ln_gain)
    half = STEPS // 2
    return pl.pallas_call(
        back_kernel,
        grid=(STEPS,),
        out_shape=[shape(64, D)] * 4 + [shape(64, WIDE)] * 2 + [shape(128, WIDE // 2)] * 2,
        in_specs=[pl.BlockSpec(one.shape, lambda at: (0, 0)) for one in smalls]
        + [pl.BlockSpec((one.shape[0], SLAB), lambda at: (0, at)) for one in larges]
        + [pl.BlockSpec(gain_part.shape, lambda at: (0, 0))],
        out_specs=[pl.BlockSpec((64, SLAB), lambda at: (0, at))] * 6
        + [
            pl.BlockSpec((128, SLAB), lambda at: (0, jnp.minimum(at, half - 1))),
            pl.BlockSpec((128, SLAB), lambda at: (0, jnp.maximum(at - half, 0))),
        ],
        scratch_shapes=[pltpu.VMEM((64, 128), F32)],
        compiler_params=PARAMS,
    )(*smalls, *larges, gain_part)


def sides(ref, rows):
    return ref[rows, D : D + 128].astype(F32) + ref[rows, D + 128 :].astype(F32)


def relay_kernel(opposite, left, right, out):
    half = WIDE // 2
    cut = D - half
    rows = slice(64, 128)
    out[:, :half] = (opposite[:, :half].astype(F32) + left[rows, :].astype(F32)).astype(BF16)
    out[:, half:D] = (
        opposite[:, half:D].astype(F32) + right[rows, :cut].astype(F32)
    ).astype(BF16)
    other = right[rows, cut : cut + 128].astype(F32) + right[rows, cut + 128 :].astype(F32)
    high, low = two_parts(sides(opposite, slice(0, 64)) + other)
    out[:, D : D + 128] = high
    out[:, D + 128 :] = low


def relay(opposite, left, right):
    return pl.pallas_call(
        relay_kernel, out_shape=shape(64, WIDE), in_specs=[VMEM] * 3, out_specs=VMEM
    )(opposite, left, right)


FAR_WIDE = D + 8 * 128
LAST_WIDE = D + 16 * 128


def spread_kernel(kept, left, right, relayed, got, *outs):
    half = WIDE // 2
    cut = D - half
    high, low = two_parts(sides(relayed, slice(0, 64)) + sides(got, slice(0, 64)))
    for at in range(4):
        rows = slice(16 * at, 16 * at + 16)
        near = kept[rows, :half].astype(F32) + left[rows, :].astype(F32)
        outs[at][:, :half] = (near + got[rows, :half].astype(F32)).astype(BF16)
        near = kept[rows, half:D].astype(F32) + right[rows, :cut].astype(F32)
        outs[at][:, half:D] = (near + got[rows, half:D].astype(F32)).astype(BF16)
        for k in range(4):
            left_edge = D + 128 * k
            outs[at][:, left_edge : left_edge + 128] = high[16 * k : 16 * k + 16]
            outs[at][:, left_edge + 512 : left_edge + 640] = low[16 * k : 16 * k + 16]


def spread(kept, left, right, relayed, got):
    return pl.pallas_call(
        spread_kernel,
        out_shape=[shape(16, FAR_WIDE)] * 4,
        in_specs=[VMEM] * 5,
        out_specs=[VMEM] * 4,
    )(kept, left, right, relayed, got)


def split_sum_kernel(*refs):
    for at in range(4):
        rows = slice(16 * at, 16 * at + 16)
        refs[4 + at][...] = total([ref[rows, :] for ref in refs[:4]]).astype(BF16)


def split_sum(parts):
    return pl.pallas_call(
        split_sum_kernel,
        out_shape=[shape(16, D)] * 4,
        in_specs=[VMEM] * 4,
        out_specs=[VMEM] * 4,
    )(*parts)


def ends_kernel(*refs):
    mixed_refs, back_refs, outs = refs[:4], refs[4:8], refs[8:]
    mixed = total([ref[...] for ref in mixed_refs])
    back = total([ref[:, :D] for ref in back_refs])
    for at in range(4):
        rows = slice(4 * at, 4 * at + 4)
        outs[at][:, :D] = jnp.concatenate([mixed[rows], back[rows]], 0).astype(BF16)
    for k in range(4):
        here = slice(D + 128 * k, D + 128 * k + 128)
        beside = slice(D + 512 + 128 * k, D + 640 + 128 * k)
        block = total([ref[:, here].astype(F32) + ref[:, beside].astype(F32) for ref in back_refs])
        for side in range(2):
            high, low = two_parts(block[8 * side : 8 * side + 8])
            edge = D + 128 * (2 * k + side)
            for out in outs:
                out[:, edge : edge + 128] = high
                out[:, edge + 1024 : edge + 1152] = low


def ends(mixed_parts, back_parts):
    return pl.pallas_call(
        ends_kernel,
        out_shape=[shape(8, LAST_WIDE)] * 4,
        in_specs=[VMEM] * 8,
        out_specs=[VMEM] * 4,
    )(*mixed_parts, *back_parts)


def finish_kernel(first, second, third, fourth, tokens, cotangent, gain, out, d_out, sums):
    parts = (first, second, third, fourth)
    rows = total([ref[:, :D] for ref in parts])
    x_float = tokens[...].astype(F32)
    scaled, inv_std = standardize(x_float)
    out[...] = (x_float + rows[:4]).astype(BF16)
    d_norm = norm_back(rows[4:], scaled, inv_std, gain[...])
    d_out[...] = (cotangent[...].astype(F32) + d_norm).astype(BF16)
    for k in range(8):
        here = slice(D + 128 * k, D + 128 * k + 128)
        beside = slice(D + 1024 + 128 * k, D + 1152 + 128 * k)
        sums[8 * k : 8 * k + 8, :] = total(
            [ref[:, here].astype(F32) + ref[:, beside].astype(F32) for ref in parts]
        )


def finish(parts, tokens, cotangent, gain):
    return pl.pallas_call(
        finish_kernel,
        out_shape=[shape(4, D), shape(4, D), shape(64, 128, dtype=F32)],
        in_specs=[VMEM] * 7,
        out_specs=[VMEM] * 3,
    )(*parts, tokens, cotangent, gain)


def grads_kernel(place, dc, ad, dc_far, ad_far, n_ref, c_ref, *refs):
    n_parts, c_parts = refs[:4], refs[4:8]
    keep, give, n_all, c_all, kept, given, sems, out_sems = refs[8:]
    half = D // 2
    own = pl.ds(pl.multiple_of(place[0] * half, half), half)
    top, low = pl.ds(0, ROWS), pl.ds(ROWS, ROWS)
    moves = [(n_ref.at[:, own], n_all.at[top]), (c_ref.at[:, own], c_all.at[top])]
    moves += n_moves(n_parts, n_all.at[low]) + c_moves(c_parts, c_all.at[low])
    loads = []
    for at, (source, target) in enumerate(moves):
        copy = pltpu.make_async_copy(source, target, sems.at[at])
        copy.start()
        loads.append(copy)
    heads = jnp.concatenate([dc[...], dc_far[...]], 0)
    units = jnp.concatenate([ad[...], ad_far[...]], 0)
    ins, half_units = 3 * HD // 2, ad.shape[1] // 2
    for copy in loads:
        copy.wait()
    stores = []
    for at, (buffer, target, column) in enumerate(
        ((given, give, 1 - place[1]), (kept, keep, place[1]))
    ):
        span = pl.ds(pl.multiple_of(column * QUARTER, QUARTER), QUARTER)
        row = 0
        for left, right in (
            (heads[:, :ins], n_all),
            (units[:, :half_units], n_all),
            (heads[:, ins:], c_all),
            (units[:, half_units:], c_all),
        ):
            height = left.shape[1]
            buffer[row : row + height, :] = row_contract(left, right[:, span]).astype(BF16)
            row += height
        copy = pltpu.make_async_copy(buffer, target, out_sems.at[at])
        copy.start()
        stores.append(copy)
    for copy in stores:
        copy.wait()


def grads(place, dc, ad, dc_far, ad_far, n_all, c_all, n_parts, c_parts):
    height = dc.shape[1] + ad.shape[1]
    return pl.pallas_call(
        grads_kernel,
        out_shape=[shape(height, QUARTER)] * 2,
        in_specs=[SMEM] + [VMEM] * 4 + [ANY] * 10,
        out_specs=[ANY] * 2,
        scratch_shapes=[
            pltpu.VMEM((2 * ROWS, D // 2), BF16),
            pltpu.VMEM((2 * ROWS, D // 2), BF16),
            pltpu.VMEM((height, QUARTER), BF16),
            pltpu.VMEM((height, QUARTER), BF16),
            pltpu.SemaphoreType.DMA((30,)),
            pltpu.SemaphoreType.DMA((2,)),
        ],
        compiler_params=PARAMS,
    )(place, dc, ad, dc_far, ad_far, n_all, c_all, *n_parts, *c_parts)


def local(tokens, cotangent, ln_gain, qk_gain, w_qkv, w_mlp_in, w_attn_out, w_mlp_out):
    tie = lax.optimization_barrier
    dp, mp = lax.axis_index("dp"), lax.axis_index("mp")
    place = jnp.stack([dp // 2, dp % 2, mp % 2]).astype(jnp.int32)
    cols, units = w_qkv.shape[1], w_mlp_in.shape[0]
    offset = mp % 2 * cols
    gains = jnp.concatenate(
        [
            lax.dynamic_slice_in_dim(qk_gain, offset, cols, 1),
            lax.dynamic_slice_in_dim(qk_gain, cols - offset, cols, 1),
        ],
        1,
    )
    gain_row = ln_gain.reshape(1, D)
    w_flat = w_qkv.reshape(3 * cols, D)

    n_rows, c_rows = apart(tie(pieces(start(tokens, cotangent, gain_row), Z)))
    n_parts, c_parts = tie((pieces(n_rows, X), pieces(c_rows, Y)))
    n_rows, c_rows, away = join(place, n_parts, c_parts)
    n_parts, c_parts, there = pieces(n_rows, Y), two_steps(c_rows), swapped(away, "dp", 2)
    n_all, c_all, qk_own, vd_own = first(n_parts, c_parts, w_flat, w_attn_out)

    qk_peer, vd_peer = swapped(qk_own, "mp", X), swapped(vd_own, "mp", X)
    there, n_next = tie((there, n_all))
    n_there, c_there = pieces(there[:64], Y), two_steps(there[64:])
    ad = hidden(n_next, c_all, w_mlp_in, w_mlp_out)
    ad_far = swapped(ad, "dp", 2)
    qk_peer, vd_peer, ad_next = tie((qk_peer, vd_peer, ad))
    dc, gain_part = head(place, qk_own, qk_peer, vd_own, vd_peer, gains)
    dc_far = swapped(dc, "dp", 2)
    outs = back(
        dc, ad_next, w_attn_out, w_mlp_out, w_flat, w_mlp_in, n_all, gain_row, gain_part
    )
    mixed = exchanged(outs[:4], Y)
    kept, opposite, left, right = outs[4:]
    left, right = swapped(left, "mp", X), swapped(right, "mp", 3 * X)
    dc_next, _ = tie((dc, kept))
    keep, give = grads(place, dc_next, ad, dc_far, ad_far, n_all, c_all, n_there, c_there)
    relayed = relay(opposite, left, right)
    got = swapped(relayed, "mp", 2 * X)
    back_parts = exchanged(spread(kept, left, right, relayed, got), Y)
    mixed = exchanged(split_sum(mixed), X)
    last = exchanged(ends(mixed, back_parts), Z)
    output, d_tokens, sums = finish(last, tokens, cotangent, gain_row)
    sums = total([sums] + [swapped(sums, "dp", step) for step in (1, 2, 3)])
    taken = swapped(give, "dp", 1)
    grad = (keep.astype(F32) + taken.astype(F32)).astype(BF16)
    edge = 3 * cols + units
    return (
        output,
        d_tokens,
        sums[:48].reshape(D),
        sums[48:50],
        grad[: 3 * cols].reshape(3, cols, QUARTER),
        grad[3 * cols : edge],
        grad[edge : edge + cols],
        grad[edge + cols :],
    )


def solution(mesh):
    return jax.shard_map(
        local,
        mesh=mesh,
        in_specs=(
            P(("dp", "mp"), None),
            P(("dp", "mp"), None),
            P(),
            P(),
            P(None, "mp", None),
            P("mp", None),
            P("mp", None),
            P("mp", None),
        ),
        out_specs=(
            P(("dp", "mp"), None),
            P(("dp", "mp"), None),
            P(),
            P(),
            P(None, "mp", "dp"),
            P("mp", "dp"),
            P("mp", "dp"),
            P("mp", "dp"),
        ),
        check_vma=False,
    )
```

```python
import functools
import math

import jax
import jax.numpy as jnp
from jax import lax
from jax.experimental import pallas as pl
from jax.experimental.pallas import tpu as pltpu
from jax.sharding import PartitionSpec as P

D = 6144
HD = 128
ROWS = 256
QUARTER = D // 4
EPS = 1e-06
X, Z, Y = 1, 4, 16
BF16 = jnp.bfloat16
F32 = jnp.float32
VMEM = pl.BlockSpec(memory_space=pltpu.VMEM)
SMEM = pl.BlockSpec(memory_space=pltpu.SMEM)
ANY = pl.BlockSpec(memory_space=pl.ANY)
PARAMS = pltpu.CompilerParams(vmem_limit_bytes=48 * 1024 * 1024)


def shape(*dims, dtype=BF16):
    return jax.ShapeDtypeStruct(dims, dtype)


def swapped(block, axis, mask):
    count = lax.axis_size(axis)
    return lax.ppermute(block, axis, [(low, low ^ mask) for low in range(count)])


def pieces(block, unit):
    return [block] + [swapped(block, "mp", step * unit) for step in (1, 2, 3)]


def exchanged(blocks, unit):
    return [blocks[0]] + [swapped(blocks[step], "mp", step * unit) for step in (1, 2, 3)]


def two_steps(block):
    half = block.shape[1] // 2
    opposite = swapped(block, "mp", 2 * X)
    pair = jnp.concatenate([block, opposite], 0)
    return [
        block,
        opposite,
        swapped(pair[:, :half], "mp", X),
        swapped(pair[:, half:], "mp", 3 * X),
    ]


def total(blocks):
    first, second, third, fourth = (block.astype(F32) for block in blocks)
    return (first + second) + (third + fourth)


def two_parts(values):
    high = values.astype(BF16)
    return high, (values - high.astype(F32)).astype(BF16)


def standardize(values):
    average = jnp.mean(values, -1, keepdims=True)
    centered = values - average
    inv_std = lax.rsqrt(jnp.mean(centered * centered, -1, keepdims=True) + EPS)
    return (centered * inv_std, inv_std)


def norm_back(gradient, scaled, inv_std, gain_row):
    weighted = gradient * gain_row
    return inv_std * (
        weighted
        - jnp.mean(weighted, -1, keepdims=True)
        - scaled * jnp.mean(weighted * scaled, -1, keepdims=True)
    )


def times_rows(left, weight):
    return lax.dot_general(left, weight, (((1,), (1,)), ((), ())), preferred_element_type=F32)


def row_contract(left, right):
    return lax.dot_general(left, right, (((0,), (0,)), ((), ())), preferred_element_type=F32)


def dot(left, right):
    return jnp.dot(left, right, preferred_element_type=F32)


def start_kernel(tokens, cotangent, gain, out):
    scaled, _ = standardize(tokens[...].astype(F32))
    both = jnp.concatenate([scaled * gain[...], cotangent[...].astype(F32)], 0)
    out[...] = both.astype(BF16)


def start(tokens, cotangent, gain):
    return pl.pallas_call(
        start_kernel,
        out_shape=shape(8, D),
        in_specs=[VMEM] * 3,
        out_specs=VMEM,
        compiler_params=PARAMS,
    )(tokens, cotangent, gain)


def apart_kernel(place, *refs):
    n_out, c_out, away = refs[4:]
    left = pl.multiple_of((1 - place[0]) * (D // 2), D // 2)
    for part, (out, rows) in enumerate(((n_out, slice(0, 16)), (c_out, slice(16, 32)))):
        half = slice(4 * part, 4 * part + 4)
        blocks = [ref[...].astype(F32)[half] for ref in refs[:4]]
        whole = jnp.concatenate(blocks, 0).astype(BF16)
        for at in range(out.shape[0] // 16):
            out[16 * at : 16 * at + 16, :] = whole
        away[rows, :] = out[0:16, pl.ds(left, D // 2)]


def apart(place, parts):
    return pl.pallas_call(
        apart_kernel,
        out_shape=[shape(16, D), shape(64, D), shape(32, D // 2)],
        in_specs=[SMEM] + [VMEM] * 4,
        out_specs=[VMEM] * 3,
        compiler_params=PARAMS,
    )(place, *parts)


def join_kernel(*refs):
    for at in range(4):
        refs[4][16 * at : 16 * at + 16, :] = refs[at][...]


def join(parts):
    return pl.pallas_call(
        join_kernel,
        out_shape=shape(64, D),
        in_specs=[VMEM] * 4,
        out_specs=VMEM,
        compiler_params=PARAMS,
    )(*parts)


def n_moves(parts, target):
    return [(parts[at], target.at[pl.ds(64 * at, 64)]) for at in range(4)]


def c_moves(place, parts, target):
    half = parts[0].shape[1] // 2
    left, right = pl.ds(0, half), pl.ds(half, half)
    moves = []
    for up in range(4):
        first = pl.multiple_of(place[23 + up], 16)
        rows, lower = pl.ds(first, 16), pl.ds(64 + first, 16)
        spots = [pl.ds(64 * up + 16 * at, 16) for at in range(4)]
        moves += [
            (parts[0].at[rows], target.at[spots[0]]),
            (parts[1].at[rows], target.at[spots[2]]),
            (parts[2].at[rows], target.at[spots[1], left]),
            (parts[2].at[lower], target.at[spots[3], left]),
            (parts[3].at[rows], target.at[spots[3], right]),
            (parts[3].at[lower], target.at[spots[1], right]),
        ]
    return moves


def first_kernel(*refs):
    place, n_parts, c_parts, weights = refs[0], refs[1:5], refs[5:9], refs[9:11]
    n_out, c_out, qk_ref, vd_ref = refs[11:15]
    n_all, c_all, wq, wo, sems = refs[15:]
    copies = []

    def begin(source, target):
        copy = pltpu.make_async_copy(source, target, sems.at[len(copies)])
        copy.start()
        copies.append(copy)
        return copy

    n_in = [begin(*move) for move in n_moves(n_parts, n_all)]
    wq_in = begin(weights[0], wq)
    c_in = [begin(*move) for move in c_moves(place, c_parts, c_all)]
    wo_in = begin(weights[1], wo)
    for copy in n_in:
        copy.wait()
    wq_in.wait()
    n_done = begin(n_all, n_out)
    cols = wo.shape[0]
    projected = jnp.zeros((ROWS, 3 * cols), F32)
    for at in range(4):
        span = slice(QUARTER * at, QUARTER * at + QUARTER)
        projected += times_rows(n_all[:, span], wq[:, span])
    qk_ref[...] = projected[:, : 2 * cols]
    for copy in c_in:
        copy.wait()
    wo_in.wait()
    c_done = begin(c_all, c_out)
    d_context = jnp.zeros((ROWS, cols), F32)
    for at in range(4):
        span = slice(QUARTER * at, QUARTER * at + QUARTER)
        d_context += times_rows(c_all[:, span], wo[:, span])
    vd_ref[...] = jnp.concatenate([projected[:, 2 * cols :], d_context], 1).astype(BF16)
    n_done.wait()
    c_done.wait()


def first(place, n_parts, c_parts, w_flat, w_out):
    cols = w_out.shape[0]
    return pl.pallas_call(
        first_kernel,
        out_shape=[
            shape(ROWS, D),
            shape(ROWS, D),
            shape(ROWS, 2 * cols, dtype=F32),
            shape(ROWS, 2 * cols),
        ],
        in_specs=[SMEM] + [ANY] * 10,
        out_specs=[ANY, ANY, VMEM, VMEM],
        scratch_shapes=[
            pltpu.VMEM((ROWS, D), BF16),
            pltpu.VMEM((ROWS, D), BF16),
            pltpu.VMEM((3 * cols, D), BF16),
            pltpu.VMEM((cols, D), BF16),
            pltpu.SemaphoreType.DMA((32,)),
        ],
        compiler_params=PARAMS,
    )(place, *n_parts, *c_parts, w_flat, w_out)


def hidden_kernel(n_ref, c_ref, win, wout, out, *scratch):
    n_all, c_all, w_in, w_out, sems = scratch
    loads = []
    for at in range(4):
        span = pl.ds(QUARTER * at, QUARTER)
        pairs = ((n_ref, n_all), (win, w_in), (c_ref, c_all), (wout, w_out))
        for which, (source, target) in enumerate(pairs):
            copy = pltpu.make_async_copy(
                source.at[:, span], target.at[:, span], sems.at[at, which]
            )
            copy.start()
            loads.append(copy)
    units = w_in.shape[0]
    hidden = jnp.zeros((ROWS, units), F32)
    d_act = jnp.zeros((ROWS, units), F32)
    for at in range(4):
        for copy in loads[4 * at : 4 * at + 4]:
            copy.wait()
        span = slice(QUARTER * at, QUARTER * at + QUARTER)
        hidden += times_rows(n_all[:, span], w_in[:, span])
        d_act += times_rows(c_all[:, span], w_out[:, span])
    cdf = 0.5 * (1.0 + lax.erf(hidden * 0.7071067811865476))
    pdf = jnp.exp(-0.5 * hidden * hidden) * 0.3989422804014327
    out[:, units:] = (hidden * cdf).astype(BF16)
    out[:, :units] = (d_act.astype(BF16).astype(F32) * (cdf + hidden * pdf)).astype(BF16)


def hidden(n_all, c_all, w_in, w_out):
    units = w_in.shape[0]
    return pl.pallas_call(
        hidden_kernel,
        out_shape=shape(ROWS, 2 * units),
        in_specs=[ANY] * 4,
        out_specs=VMEM,
        scratch_shapes=[
            pltpu.VMEM((ROWS, D), BF16),
            pltpu.VMEM((ROWS, D), BF16),
            pltpu.VMEM((units, D), BF16),
            pltpu.VMEM((units, D), BF16),
            pltpu.SemaphoreType.DMA((4, 4)),
        ],
        compiler_params=PARAMS,
    )(n_all, c_all, w_in, w_out)


def head_kernel(place, qk_own, qk_peer, vd_own, vd_peer, gains, ad, out, gain_ref):
    cols = HD // 2

    def whole(own, peer, left):
        other = jnp.concatenate(
            [peer[16 * (at ^ 1) : 16 * (at ^ 1) + 16, :] for at in range(ROWS // 16)], 0
        )
        return jnp.concatenate(
            [own[:, left : left + cols], other[:, left : left + cols]], 1
        )

    query, key = whole(qk_own, qk_peer, 0), whole(qk_own, qk_peer, cols)
    values, d_ctx = whole(vd_own, vd_peer, 0), whole(vd_own, vd_peer, cols)
    q_gain, k_gain = gains[0:1, :], gains[1:2, :]
    q_scaled, q_inv = standardize(query)
    k_scaled, k_inv = standardize(key)
    q_normed = (q_scaled * q_gain).astype(BF16)
    k_normed = (k_scaled * k_gain).astype(BF16)
    scores = times_rows(q_normed, k_normed) * (1.0 / math.sqrt(HD))
    grown = jnp.exp(scores - jnp.max(scores, -1, keepdims=True))
    probs = (grown / jnp.sum(grown, -1, keepdims=True)).astype(BF16)
    context = dot(probs, values)[:, :cols]
    d_probs = times_rows(d_ctx, values)
    probs_f = probs.astype(F32)
    centered = d_probs - jnp.sum(probs_f * d_probs, -1, keepdims=True)
    d_scores = (probs_f * centered * (1.0 / math.sqrt(HD))).astype(BF16)
    d_values = row_contract(probs, d_ctx)
    d_qn = dot(d_scores, k_normed)
    d_kn = row_contract(d_scores, q_normed)
    d_query = norm_back(d_qn, q_scaled, q_inv, q_gain)
    d_key = norm_back(d_kn, k_scaled, k_inv, k_gain)
    out[:, :HD] = jnp.concatenate([d_query[:, :cols], d_key[:, :cols]], 1).astype(BF16)
    out[:, HD : 2 * HD] = jnp.concatenate([d_values[:, :cols], context], 1).astype(BF16)
    out[:, 2 * HD :] = ad[...]
    for row, terms in enumerate((d_qn * q_scaled, d_kn * k_scaled)):
        mine = jnp.sum(terms, 0, keepdims=True)[:, :cols]
        none = jnp.zeros_like(mine)
        even = jnp.concatenate([mine, none], 1)
        odd = jnp.concatenate([none, mine], 1)
        gain_ref[row : row + 1, :] = jnp.where(place[2] == 0, even, odd)


def head(place, qk_own, qk_peer, vd_own, vd_peer, gains, ad):
    return pl.pallas_call(
        head_kernel,
        out_shape=[shape(ROWS, 2 * HD + ad.shape[1]), shape(2, HD, dtype=F32)],
        in_specs=[SMEM] + [VMEM] * 6,
        out_specs=[VMEM] * 2,
        compiler_params=PARAMS,
    )(place, qk_own, qk_peer, vd_own, vd_peer, gains, ad)


SLAB = 1024
STEPS = D // SLAB


def back_kernel(acts, w_ao, w_mo, w_qkv, w_mi, n_ref, gain, gain_part, *outs):
    mix_outs, kept, opposite, near_left, near_right, sums = outs[:4], *outs[4:]
    at = pl.program_id(0)
    ins, units, heads = w_qkv.shape[0], w_mi.shape[0], 2 * HD
    d_norm = dot(acts[:, :ins], w_qkv[...]) + dot(acts[:, heads : heads + units], w_mi[...])
    part = jnp.sum(d_norm * n_ref[...].astype(F32), 0, keepdims=True) / gain[...]

    @pl.when(at == 0)
    def _():
        sums[48:64, :] = jnp.zeros((16, 128), F32)
        sums[48:50, :] = gain_part[...]

    for k in range(SLAB // 128):
        sums[pl.ds(SLAB // 128 * at + k, 1), :] = part[:, 128 * k : 128 * k + 128]

    chunks = [
        jnp.concatenate(
            [d_norm[64 * up + 16 * k : 64 * up + 16 * k + 16] for up in range(4)], 0
        ).astype(BF16)
        for k in range(4)
    ]
    kept[...] = chunks[0]
    opposite[...] = chunks[2]

    @pl.when(at < STEPS // 2)
    def _():
        near_left[:64, :] = chunks[1]
        near_left[64:, :] = chunks[3]

    @pl.when(at >= STEPS // 2)
    def _():
        near_right[:64, :] = chunks[3]
        near_right[64:, :] = chunks[1]

    mixed = dot(acts[:, ins:heads], w_ao[...]) + dot(acts[:, heads + units :], w_mo[...])
    for k in range(4):
        mix_outs[k][...] = mixed[64 * k : 64 * k + 64].astype(BF16)


def back(acts, w_ao, w_mo, w_qkv, w_mi, n_all, ln_gain, gain_part):
    larges = (w_ao, w_mo, w_qkv, w_mi, n_all, ln_gain)
    half = STEPS // 2
    return pl.pallas_call(
        back_kernel,
        grid=(STEPS,),
        out_shape=[shape(64, D)] * 6
        + [shape(128, D // 2)] * 2
        + [shape(64, 128, dtype=F32)],
        in_specs=[pl.BlockSpec(acts.shape, lambda at: (0, 0))]
        + [pl.BlockSpec((one.shape[0], SLAB), lambda at: (0, at)) for one in larges]
        + [pl.BlockSpec(gain_part.shape, lambda at: (0, 0))],
        out_specs=[pl.BlockSpec((64, SLAB), lambda at: (0, at))] * 6
        + [
            pl.BlockSpec((128, SLAB), lambda at: (0, jnp.minimum(at, half - 1))),
            pl.BlockSpec((128, SLAB), lambda at: (0, jnp.maximum(at - half, 0))),
            pl.BlockSpec((64, 128), lambda at: (0, 0)),
        ],
        compiler_params=PARAMS,
    )(acts, *larges, gain_part)


def pack_kernel(acts, sums, other, out):
    out[:ROWS, :] = acts[...]
    high, low = two_parts(sums[...] + other[...])
    for side in range(2):
        rows = slice(32 * side, 32 * side + 32)
        out[ROWS:, 128 * side : 128 * side + 128] = high[rows]
        out[ROWS:, 256 + 128 * side : 384 + 128 * side] = low[rows]
    out[ROWS:, 512:] = jnp.zeros((32, 256), BF16)


def pack(acts, sums, other):
    return pl.pallas_call(
        pack_kernel,
        out_shape=shape(ROWS + 32, acts.shape[1]),
        in_specs=[VMEM] * 3,
        out_specs=VMEM,
        compiler_params=PARAMS,
    )(acts, sums, other)


def relay_kernel(opposite, left, right, packed, packed_far, out, rounded):
    half = D // 2
    rows = slice(64, 128)
    out[:, :half] = (opposite[:, :half].astype(F32) + left[rows, :].astype(F32)).astype(BF16)
    out[:, half:D] = (opposite[:, half:].astype(F32) + right[rows, :].astype(F32)).astype(BF16)
    for side in range(2):
        here = slice(128 * side, 128 * side + 128)
        beside = slice(256 + 128 * side, 384 + 128 * side)
        mine, theirs = (
            ref[ROWS:, here].astype(F32) + ref[ROWS:, beside].astype(F32)
            for ref in (packed, packed_far)
        )
        high, low = two_parts(mine + theirs)
        rows = slice(32 * side, 32 * side + 32)
        out[rows, D : D + 128] = high
        out[rows, D + 128 :] = low
        rounded[rows, :] = high.astype(F32) + low.astype(F32)


def relay(opposite, left, right, packed, packed_far):
    return pl.pallas_call(
        relay_kernel,
        out_shape=[shape(64, D + 256), shape(64, 128, dtype=F32)],
        in_specs=[VMEM] * 5,
        out_specs=[VMEM] * 2,
        compiler_params=PARAMS,
    )(opposite, left, right, packed, packed_far)


FAR_WIDE = D + 8 * 128
LAST_WIDE = D + 16 * 128


def spread_kernel(kept, left, right, got, sums, near, far, *outs):
    half = D // 2
    other = got[:, D : D + 128].astype(F32) + got[:, D + 128 :].astype(F32)
    high, low = two_parts((sums[...] + near[...]) + (other + far[...]))
    for at in range(4):
        rows = slice(16 * at, 16 * at + 16)
        first = kept[rows, :half].astype(F32) + left[rows, :].astype(F32)
        outs[at][:, :half] = (first + got[rows, :half].astype(F32)).astype(BF16)
        first = kept[rows, half:].astype(F32) + right[rows, :].astype(F32)
        outs[at][:, half:D] = (first + got[rows, half:D].astype(F32)).astype(BF16)
        for k in range(4):
            left_edge = D + 128 * k
            outs[at][:, left_edge : left_edge + 128] = high[16 * k : 16 * k + 16]
            outs[at][:, left_edge + 512 : left_edge + 640] = low[16 * k : 16 * k + 16]


def spread(*parts):
    return pl.pallas_call(
        spread_kernel,
        out_shape=[shape(16, FAR_WIDE)] * 4,
        in_specs=[VMEM] * 7,
        out_specs=[VMEM] * 4,
        compiler_params=PARAMS,
    )(*parts)


def split_sum_kernel(place, *refs):
    for at in range(4):
        rows = slice(16 * at, 16 * at + 16)
        spot = pl.ds(pl.multiple_of(place[19 + at], 16), 16)
        refs[4][spot, :] = total([ref[rows, :] for ref in refs[:4]]).astype(BF16)


def split_sum(place, parts):
    return pl.pallas_call(
        split_sum_kernel,
        out_shape=shape(64, D),
        in_specs=[SMEM] + [VMEM] * 4,
        out_specs=VMEM,
        compiler_params=PARAMS,
    )(place, *parts)


def ends_kernel(*refs):
    mixed_ref, back_refs, outs = refs[0], refs[1:5], refs[5:]
    mixed = total([mixed_ref[16 * at : 16 * at + 16, :] for at in range(4)])
    back = total([ref[:, :D] for ref in back_refs])
    for at in range(4):
        rows = slice(4 * at, 4 * at + 4)
        outs[at][:, :D] = jnp.concatenate([mixed[rows], back[rows]], 0).astype(BF16)
    for k in range(4):
        here = slice(D + 128 * k, D + 128 * k + 128)
        beside = slice(D + 512 + 128 * k, D + 640 + 128 * k)
        block = total([ref[:, here].astype(F32) + ref[:, beside].astype(F32) for ref in back_refs])
        for side in range(2):
            high, low = two_parts(block[8 * side : 8 * side + 8])
            edge = D + 128 * (2 * k + side)
            for out in outs:
                out[:, edge : edge + 128] = high
                out[:, edge + 1024 : edge + 1152] = low


def ends(mixed, back_parts):
    return pl.pallas_call(
        ends_kernel,
        out_shape=[shape(8, LAST_WIDE)] * 4,
        in_specs=[VMEM] * 5,
        out_specs=[VMEM] * 4,
        compiler_params=PARAMS,
    )(mixed, *back_parts)


def finish_kernel(first, second, third, fourth, tokens, cotangent, gain, out, d_out, ln_out, qk_out):
    parts = (first, second, third, fourth)
    rows = total([ref[:, :D] for ref in parts])
    x_float = tokens[...].astype(F32)
    scaled, inv_std = standardize(x_float)
    out[...] = (x_float + rows[:4]).astype(BF16)
    d_norm = norm_back(rows[4:], scaled, inv_std, gain[...])
    d_out[...] = (cotangent[...].astype(F32) + d_norm).astype(BF16)
    for k in range(8):
        here = slice(D + 128 * k, D + 128 * k + 128)
        beside = slice(D + 1024 + 128 * k, D + 1152 + 128 * k)
        block = total([ref[:, here].astype(F32) + ref[:, beside].astype(F32) for ref in parts])
        if k < 6:
            for row in range(8):
                edge = 128 * (8 * k + row)
                ln_out[:, edge : edge + 128] = block[row : row + 1]
        if k == 6:
            qk_out[...] = block[:2]


def finish(parts, tokens, cotangent, gain):
    return pl.pallas_call(
        finish_kernel,
        out_shape=[
            shape(4, D),
            shape(4, D),
            shape(1, D, dtype=F32),
            shape(2, HD, dtype=F32),
        ],
        in_specs=[VMEM] * 7,
        out_specs=[VMEM] * 4,
        compiler_params=PARAMS,
    )(*parts, tokens, cotangent, gain)


def add_kernel(keep, taken, *outs):
    row = 0
    for out in outs:
        rows = slice(row, row + out.shape[0])
        out[...] = (keep[rows, :].astype(F32) + taken[rows, :].astype(F32)).astype(BF16)
        row += out.shape[0]


def add(keep, taken, heights):
    width = QUARTER // 2
    return pl.pallas_call(
        add_kernel,
        grid=(2,),
        out_shape=[shape(height, QUARTER) for height in heights],
        in_specs=[pl.BlockSpec((keep.shape[0], width), lambda at: (0, at))] * 2,
        out_specs=[pl.BlockSpec((height, width), lambda at: (0, at)) for height in heights],
    )(keep, taken)


def grads_kernel(place, acts, acts_far, n_ref, c_ref, far, *refs):
    keep, give, n_all, c_all, kept, given, sems, out_sems = refs
    half = D // 2
    own = pl.ds(pl.multiple_of(place[0] * half, half), half)
    top = pl.ds(0, ROWS)
    moves = [(n_ref.at[:, own], n_all.at[top]), (c_ref.at[:, own], c_all.at[top])]
    for at in range(16):
        row = pl.multiple_of(place[3 + at], 32)
        spot = pl.ds(ROWS + 16 * at, 16)
        moves.append((far.at[pl.ds(row, 16)], n_all.at[spot]))
        moves.append((far.at[pl.ds(row + 16, 16)], c_all.at[spot]))
    loads = []
    for at, (source, target) in enumerate(moves):
        copy = pltpu.make_async_copy(source, target, sems.at[at])
        copy.start()
        loads.append(copy)
    whole = jnp.concatenate([acts[:ROWS, :], acts_far[:ROWS, :]], 0)
    ins, heads = 3 * HD // 2, 2 * HD
    units = (whole.shape[1] - heads) // 2
    for copy in loads:
        copy.wait()
    stores = []
    for at, (buffer, target, column) in enumerate(
        ((given, give, 1 - place[1]), (kept, keep, place[1]))
    ):
        span = pl.ds(pl.multiple_of(column * QUARTER, QUARTER), QUARTER)
        row = 0
        for left, right in (
            (whole[:, :ins], n_all),
            (whole[:, heads : heads + units], n_all),
            (whole[:, ins:heads], c_all),
            (whole[:, heads + units :], c_all),
        ):
            height = left.shape[1]
            buffer[row : row + height, :] = row_contract(left, right[:, span]).astype(BF16)
            row += height
        copy = pltpu.make_async_copy(buffer, target, out_sems.at[at])
        copy.start()
        stores.append(copy)
    for copy in stores:
        copy.wait()


def grads(place, acts, acts_far, n_all, c_all, far):
    height = acts.shape[1]
    return pl.pallas_call(
        grads_kernel,
        out_shape=[shape(height, QUARTER)] * 2,
        in_specs=[SMEM] + [VMEM] * 2 + [ANY] * 3,
        out_specs=[ANY] * 2,
        scratch_shapes=[
            pltpu.VMEM((2 * ROWS, D // 2), BF16),
            pltpu.VMEM((2 * ROWS, D // 2), BF16),
            pltpu.VMEM((height, QUARTER), BF16),
            pltpu.VMEM((height, QUARTER), BF16),
            pltpu.SemaphoreType.DMA((34,)),
            pltpu.SemaphoreType.DMA((2,)),
        ],
        compiler_params=PARAMS,
    )(place, acts, acts_far, n_all, c_all, far)


def all_to_all(block, unit):
    groups = [
        [first + unit * at for at in range(4)]
        for first in range(64)
        if first // unit % 4 == 0
    ]
    return lax.all_to_all(block, "mp", 0, 0, axis_index_groups=groups, tiled=True)


def all_planes(block):
    planes = [[Y * up + Z * deep + X * at for up in range(4) for at in range(4)] for deep in range(4)]
    return lax.all_gather(block, "mp", axis=0, tiled=True, axis_index_groups=planes)


def local(tokens, cotangent, ln_gain, qk_gain, w_qkv, w_mlp_in, w_attn_out, w_mlp_out):
    tie = lax.optimization_barrier
    dp, mp = lax.axis_index("dp"), lax.axis_index("mp")
    up, at = mp // Y, mp % 4
    starts = [32 * (4 * (up ^ high) + (at ^ low)) for high in range(4) for low in range(4)]
    starts += [16 * (at ^ step) for step in range(4)] + [16 * (up ^ step) for step in range(4)]
    place = jnp.stack([dp // 2, dp % 2, mp % 2] + starts).astype(jnp.int32)
    cols, units = w_qkv.shape[1], w_mlp_in.shape[0]
    offset = mp % 2 * cols
    gains = jnp.concatenate(
        [
            lax.dynamic_slice_in_dim(qk_gain, offset, cols, 1),
            lax.dynamic_slice_in_dim(qk_gain, cols - offset, cols, 1),
        ],
        1,
    )
    gain_row = ln_gain.reshape(1, D)
    w_flat = w_qkv.reshape(3 * cols, D)

    n_rows, c_rows, away = apart(place, tie(pieces(start(tokens, cotangent, gain_row), Z)))
    n_parts, c_rows = tie((pieces(n_rows, X), all_to_all(c_rows, Y)))
    n_rows = join(n_parts)
    n_rows, c_rows, away = tie((n_rows, c_rows, away))
    n_parts, c_parts, there = tie((pieces(n_rows, Y), two_steps(c_rows), swapped(away, "dp", 2)))
    n_all, c_all, qk_own, vd_own = first(place, n_parts, c_parts, w_flat, w_attn_out)

    qk_peer, vd_peer = swapped(qk_own, "mp", X), swapped(vd_own, "mp", X)
    there, n_next = tie((there, n_all))
    far = all_planes(there)
    ad = hidden(n_next, c_all, w_mlp_in, w_mlp_out)
    qk_peer, vd_peer, ad = tie((qk_peer, vd_peer, ad))
    acts, gain_part = head(place, qk_own, qk_peer, vd_own, vd_peer, gains, ad)
    outs = back(acts, w_attn_out, w_mlp_out, w_flat, w_mlp_in, n_all, gain_row, gain_part)
    kept, opposite, left, right, sums = outs[4:]
    left, right = swapped(left, "mp", X), swapped(right, "mp", 3 * X)
    near, late = swapped(outs[1], "mp", Y), swapped(outs[3], "mp", 3 * Y)
    packed = pack(acts, sums, swapped(sums, "dp", 1))
    packed_far = swapped(packed, "dp", 2)
    left, right, near, late, packed_far = tie((left, right, near, late, packed_far))
    relayed, sums = relay(opposite, left, right, packed, packed_far)
    relayed, middle, packed_far = tie((relayed, outs[2], packed_far))
    got, middle = swapped(relayed, "mp", 2 * X), swapped(middle, "mp", 2 * Y)
    other_sums = swapped(sums, "mp", X), swapped(sums, "mp", 3 * X)
    keep, give = grads(place, packed, packed_far, n_all, c_all, far)
    got, middle, other_sums, keep, give = tie((got, middle, other_sums, keep, give))
    taken = swapped(give, "dp", 1)
    spreads = spread(kept, left, right, got, sums, *other_sums)
    spreads, middle = tie((spreads, middle))
    back_parts = exchanged(spreads, Y)
    mixed = all_to_all(split_sum(place, [outs[0], near, middle, late]), X)
    last = exchanged(ends(mixed, back_parts), Z)
    parts = add(keep, taken, (3 * cols, units, cols, units))
    last, parts = tie((last, parts))
    output, d_tokens, g_ln, g_qk = finish(last, tokens, cotangent, gain_row)
    return (
        output,
        d_tokens,
        g_ln.reshape(D),
        g_qk,
        parts[0].reshape(3, cols, QUARTER),
        *parts[1:],
    )


def solution(mesh):
    return jax.shard_map(
        local,
        mesh=mesh,
        in_specs=(
            P(("dp", "mp"), None),
            P(("dp", "mp"), None),
            P(),
            P(),
            P(None, "mp", None),
            P("mp", None),
            P("mp", None),
            P("mp", None),
        ),
        out_specs=(
            P(("dp", "mp"), None),
            P(("dp", "mp"), None),
            P(),
            P(),
            P(None, "mp", "dp"),
            P("mp", "dp"),
            P("mp", "dp"),
            P("mp", "dp"),
        ),
        check_vma=False,
    )
```

```python
import functools
import math

import jax
import jax.numpy as jnp
from jax import lax
from jax.experimental import pallas as pl
from jax.experimental.pallas import tpu as pltpu
from jax.sharding import PartitionSpec as P

D = 6144
HD = 128
ROWS = 256
QUARTER = D // 4
EPS = 1e-06
X, Z, Y = 1, 4, 16
BF16 = jnp.bfloat16
F32 = jnp.float32
VMEM = pl.BlockSpec(memory_space=pltpu.VMEM)
SMEM = pl.BlockSpec(memory_space=pltpu.SMEM)
ANY = pl.BlockSpec(memory_space=pl.ANY)
PARAMS = pltpu.CompilerParams(vmem_limit_bytes=48 * 1024 * 1024)


def shape(*dims, dtype=BF16):
    return jax.ShapeDtypeStruct(dims, dtype)


def swapped(block, axis, mask):
    count = lax.axis_size(axis)
    return lax.ppermute(block, axis, [(low, low ^ mask) for low in range(count)])


def pieces(block, unit):
    return [block] + [swapped(block, "mp", step * unit) for step in (1, 2, 3)]


def exchanged(blocks, unit):
    return [blocks[0]] + [swapped(blocks[step], "mp", step * unit) for step in (1, 2, 3)]


def two_steps(block):
    half = block.shape[1] // 2
    opposite = swapped(block, "mp", 2 * X)
    pair = jnp.concatenate([block, opposite], 0)
    return [
        block,
        opposite,
        swapped(pair[:, :half], "mp", X),
        swapped(pair[:, half:], "mp", 3 * X),
    ]


def total(blocks):
    first, second, third, fourth = (block.astype(F32) for block in blocks)
    return (first + second) + (third + fourth)


def two_parts(values):
    high = values.astype(BF16)
    return high, (values - high.astype(F32)).astype(BF16)


def standardize(values):
    average = jnp.mean(values, -1, keepdims=True)
    centered = values - average
    inv_std = lax.rsqrt(jnp.mean(centered * centered, -1, keepdims=True) + EPS)
    return (centered * inv_std, inv_std)


def norm_back(gradient, scaled, inv_std, gain_row):
    weighted = gradient * gain_row
    return inv_std * (
        weighted
        - jnp.mean(weighted, -1, keepdims=True)
        - scaled * jnp.mean(weighted * scaled, -1, keepdims=True)
    )


def times_rows(left, weight):
    return lax.dot_general(left, weight, (((1,), (1,)), ((), ())), preferred_element_type=F32)


def row_contract(left, right):
    return lax.dot_general(left, right, (((0,), (0,)), ((), ())), preferred_element_type=F32)


def dot(left, right):
    return jnp.dot(left, right, preferred_element_type=F32)


def start_kernel(tokens, cotangent, gain, out):
    scaled, _ = standardize(tokens[...].astype(F32))
    both = jnp.concatenate([scaled * gain[...], cotangent[...].astype(F32)], 0)
    out[...] = both.astype(BF16)


def start(tokens, cotangent, gain):
    return pl.pallas_call(
        start_kernel,
        grid=(1,),
        out_shape=shape(8, D),
        in_specs=[pl.BlockSpec((rows, D), lambda at: (0, 0)) for rows in (4, 4, 1)],
        out_specs=pl.BlockSpec((8, D), lambda at: (0, 0)),
        compiler_params=PARAMS,
    )(tokens, cotangent, gain)


def apart_kernel(place, *refs):
    n_out, c_out, away = refs[4:]
    left = pl.multiple_of((1 - place[0]) * (D // 2), D // 2)
    for part, (out, rows) in enumerate(((n_out, slice(0, 16)), (c_out, slice(16, 32)))):
        half = slice(4 * part, 4 * part + 4)
        blocks = [ref[...].astype(F32)[half] for ref in refs[:4]]
        whole = jnp.concatenate(blocks, 0).astype(BF16)
        for at in range(out.shape[0] // 16):
            out[16 * at : 16 * at + 16, :] = whole
        away[rows, :] = out[0:16, pl.ds(left, D // 2)]


def apart(place, parts):
    return pl.pallas_call(
        apart_kernel,
        out_shape=[shape(16, D), shape(64, D), shape(32, D // 2)],
        in_specs=[SMEM] + [VMEM] * 4,
        out_specs=[VMEM] * 3,
        compiler_params=PARAMS,
    )(place, *parts)


def join_kernel(*refs):
    for at in range(4):
        refs[4][16 * at : 16 * at + 16, :] = refs[at][...]


def join(parts):
    return pl.pallas_call(
        join_kernel,
        out_shape=shape(64, D),
        in_specs=[VMEM] * 4,
        out_specs=VMEM,
        compiler_params=PARAMS,
    )(*parts)


def n_moves(parts, target):
    return [(parts[at], target.at[pl.ds(64 * at, 64)]) for at in range(4)]


def c_moves(place, parts, target):
    half = parts[0].shape[1] // 2
    left, right = pl.ds(0, half), pl.ds(half, half)
    moves = []
    for up in range(4):
        first = pl.multiple_of(place[23 + up], 16)
        rows, lower = pl.ds(first, 16), pl.ds(64 + first, 16)
        spots = [pl.ds(64 * up + 16 * at, 16) for at in range(4)]
        moves += [
            (parts[0].at[rows], target.at[spots[0]]),
            (parts[1].at[rows], target.at[spots[2]]),
            (parts[2].at[rows], target.at[spots[1], left]),
            (parts[2].at[lower], target.at[spots[3], left]),
            (parts[3].at[rows], target.at[spots[3], right]),
            (parts[3].at[lower], target.at[spots[1], right]),
        ]
    return moves


def first_kernel(*refs):
    place, n_parts, c_parts, weights = refs[0], refs[1:5], refs[5:9], refs[9:11]
    n_out, c_out, qk_ref, send_ref = refs[11:15]
    n_all, c_all, wq, wo, sems = refs[15:]
    copies = []

    def begin(source, target):
        copy = pltpu.make_async_copy(source, target, sems.at[len(copies)])
        copy.start()
        copies.append(copy)
        return copy

    n_in = [begin(*move) for move in n_moves(n_parts, n_all)]
    wq_in = begin(weights[0], wq)
    c_in = [begin(*move) for move in c_moves(place, c_parts, c_all)]
    wo_in = begin(weights[1], wo)
    for copy in n_in:
        copy.wait()
    wq_in.wait()
    n_done = begin(n_all, n_out)
    cols = wo.shape[0]
    projected = jnp.zeros((ROWS, 3 * cols), F32)
    for at in range(4):
        span = slice(QUARTER * at, QUARTER * at + QUARTER)
        projected += times_rows(n_all[:, span], wq[:, span])
    queries = projected[:, : 2 * cols]
    qk_ref[...] = queries
    send_ref[:, : 2 * cols], send_ref[:, 2 * cols : 4 * cols] = two_parts(queries)
    for copy in c_in:
        copy.wait()
    wo_in.wait()
    c_done = begin(c_all, c_out)
    d_context = jnp.zeros((ROWS, cols), F32)
    for at in range(4):
        span = slice(QUARTER * at, QUARTER * at + QUARTER)
        d_context += times_rows(c_all[:, span], wo[:, span])
    values = projected[:, 2 * cols :]
    send_ref[:, 4 * cols :] = jnp.concatenate([values, d_context], 1).astype(BF16)
    n_done.wait()
    c_done.wait()


def first(place, n_parts, c_parts, w_flat, w_out):
    cols = w_out.shape[0]
    return pl.pallas_call(
        first_kernel,
        out_shape=[
            shape(ROWS, D),
            shape(ROWS, D),
            shape(ROWS, 2 * cols, dtype=F32),
            shape(ROWS, 6 * cols),
        ],
        in_specs=[SMEM] + [ANY] * 10,
        out_specs=[ANY, ANY, VMEM, VMEM],
        scratch_shapes=[
            pltpu.VMEM((ROWS, D), BF16),
            pltpu.VMEM((ROWS, D), BF16),
            pltpu.VMEM((3 * cols, D), BF16),
            pltpu.VMEM((cols, D), BF16),
            pltpu.SemaphoreType.DMA((32,)),
        ],
        compiler_params=PARAMS,
    )(place, *n_parts, *c_parts, w_flat, w_out)


def hidden_kernel(n_ref, c_ref, win, wout, out, *scratch):
    n_all, c_all, w_in, w_out, sems = scratch
    loads = []
    for at in range(4):
        span = pl.ds(QUARTER * at, QUARTER)
        pairs = ((n_ref, n_all), (win, w_in), (c_ref, c_all), (wout, w_out))
        for which, (source, target) in enumerate(pairs):
            copy = pltpu.make_async_copy(
                source.at[:, span], target.at[:, span], sems.at[at, which]
            )
            copy.start()
            loads.append(copy)
    units = w_in.shape[0]
    hidden = jnp.zeros((ROWS, units), F32)
    d_act = jnp.zeros((ROWS, units), F32)
    for at in range(4):
        for copy in loads[4 * at : 4 * at + 4]:
            copy.wait()
        span = slice(QUARTER * at, QUARTER * at + QUARTER)
        hidden += times_rows(n_all[:, span], w_in[:, span])
        d_act += times_rows(c_all[:, span], w_out[:, span])
    cdf = 0.5 * (1.0 + lax.erf(hidden * 0.7071067811865476))
    pdf = jnp.exp(-0.5 * hidden * hidden) * 0.3989422804014327
    out[:, units:] = (hidden * cdf).astype(BF16)
    out[:, :units] = (d_act.astype(BF16).astype(F32) * (cdf + hidden * pdf)).astype(BF16)


def hidden(n_all, c_all, w_in, w_out):
    units = w_in.shape[0]
    return pl.pallas_call(
        hidden_kernel,
        out_shape=shape(ROWS, 2 * units),
        in_specs=[ANY] * 4,
        out_specs=VMEM,
        scratch_shapes=[
            pltpu.VMEM((ROWS, D), BF16),
            pltpu.VMEM((ROWS, D), BF16),
            pltpu.VMEM((units, D), BF16),
            pltpu.VMEM((units, D), BF16),
            pltpu.SemaphoreType.DMA((4, 4)),
        ],
        compiler_params=PARAMS,
    )(n_all, c_all, w_in, w_out)


def head_kernel(place, qk_own, own, peer, gains, ad, out, gain_ref):
    cols = HD // 2
    other = jnp.concatenate(
        [peer[16 * (at ^ 1) : 16 * (at ^ 1) + 16, :] for at in range(ROWS // 16)], 0
    )
    qk_other = other[:, :HD].astype(F32) + other[:, HD : 2 * HD].astype(F32)
    query = jnp.concatenate([qk_own[:, :cols], qk_other[:, :cols]], 1)
    key = jnp.concatenate([qk_own[:, cols:], qk_other[:, cols:]], 1)
    left, right = slice(2 * HD, 2 * HD + cols), slice(2 * HD + cols, 3 * HD)
    values = jnp.concatenate([own[:, left], other[:, left]], 1)
    d_ctx = jnp.concatenate([own[:, right], other[:, right]], 1)
    q_gain, k_gain = gains[0:1, :], gains[1:2, :]
    q_scaled, q_inv = standardize(query)
    k_scaled, k_inv = standardize(key)
    q_normed = (q_scaled * q_gain).astype(BF16)
    k_normed = (k_scaled * k_gain).astype(BF16)
    scores = times_rows(q_normed, k_normed) * (1.0 / math.sqrt(HD))
    grown = jnp.exp(scores - jnp.max(scores, -1, keepdims=True))
    probs = (grown / jnp.sum(grown, -1, keepdims=True)).astype(BF16)
    context = dot(probs, values)[:, :cols]
    d_probs = times_rows(d_ctx, values)
    probs_f = probs.astype(F32)
    centered = d_probs - jnp.sum(probs_f * d_probs, -1, keepdims=True)
    d_scores = (probs_f * centered * (1.0 / math.sqrt(HD))).astype(BF16)
    d_values = row_contract(probs, d_ctx)
    d_qn = dot(d_scores, k_normed)
    d_kn = row_contract(d_scores, q_normed)
    d_query = norm_back(d_qn, q_scaled, q_inv, q_gain)
    d_key = norm_back(d_kn, k_scaled, k_inv, k_gain)
    out[:, :HD] = jnp.concatenate([d_query[:, :cols], d_key[:, :cols]], 1).astype(BF16)
    out[:, HD : 2 * HD] = jnp.concatenate([d_values[:, :cols], context], 1).astype(BF16)
    out[:, 2 * HD :] = ad[...]
    for row, terms in enumerate((d_qn * q_scaled, d_kn * k_scaled)):
        mine = jnp.sum(terms, 0, keepdims=True)[:, :cols]
        none = jnp.zeros_like(mine)
        even = jnp.concatenate([mine, none], 1)
        odd = jnp.concatenate([none, mine], 1)
        gain_ref[row : row + 1, :] = jnp.where(place[2] == 0, even, odd)


def head(place, qk_own, own, peer, gains, ad):
    return pl.pallas_call(
        head_kernel,
        out_shape=[shape(ROWS, 2 * HD + ad.shape[1]), shape(2, HD, dtype=F32)],
        in_specs=[SMEM] + [VMEM] * 5,
        out_specs=[VMEM] * 2,
        compiler_params=PARAMS,
    )(place, qk_own, own, peer, gains, ad)


SLAB = 1536
STEPS = D // SLAB


def back_kernel(acts, w_ao, w_mo, w_qkv, w_mi, n_ref, gain, gain_part, *outs):
    mix_outs, kept, opposite, near_left, near_right, sums = outs[:4], *outs[4:]
    at = pl.program_id(0)
    ins, units, heads = w_qkv.shape[0], w_mi.shape[0], 2 * HD
    d_norm = dot(acts[:, :ins], w_qkv[...]) + dot(acts[:, heads : heads + units], w_mi[...])
    part = jnp.sum(d_norm * n_ref[...].astype(F32), 0, keepdims=True) / gain[...]

    @pl.when(at == 0)
    def _():
        sums[48:64, :] = jnp.zeros((16, 128), F32)
        sums[48:50, :] = gain_part[...]

    for k in range(SLAB // 128):
        sums[pl.ds(SLAB // 128 * at + k, 1), :] = part[:, 128 * k : 128 * k + 128]

    chunks = [
        jnp.concatenate(
            [d_norm[64 * up + 16 * k : 64 * up + 16 * k + 16] for up in range(4)], 0
        ).astype(BF16)
        for k in range(4)
    ]
    kept[...] = chunks[0]
    opposite[...] = chunks[2]

    @pl.when(at < STEPS // 2)
    def _():
        near_left[:64, :] = chunks[1]
        near_left[64:, :] = chunks[3]

    @pl.when(at >= STEPS // 2)
    def _():
        near_right[:64, :] = chunks[3]
        near_right[64:, :] = chunks[1]

    mixed = dot(acts[:, ins:heads], w_ao[...]) + dot(acts[:, heads + units :], w_mo[...])
    for k in range(4):
        mix_outs[k][...] = mixed[64 * k : 64 * k + 64].astype(BF16)


def back(acts, w_ao, w_mo, w_qkv, w_mi, n_all, ln_gain, gain_part):
    larges = (w_ao, w_mo, w_qkv, w_mi, n_all, ln_gain)
    half = STEPS // 2
    return pl.pallas_call(
        back_kernel,
        grid=(STEPS,),
        out_shape=[shape(64, D)] * 6
        + [shape(128, D // 2)] * 2
        + [shape(64, 128, dtype=F32)],
        in_specs=[pl.BlockSpec(acts.shape, lambda at: (0, 0))]
        + [pl.BlockSpec((one.shape[0], SLAB), lambda at: (0, at)) for one in larges]
        + [pl.BlockSpec(gain_part.shape, lambda at: (0, 0))],
        out_specs=[pl.BlockSpec((64, SLAB), lambda at: (0, at))] * 6
        + [
            pl.BlockSpec((128, SLAB), lambda at: (0, jnp.minimum(at, half - 1))),
            pl.BlockSpec((128, SLAB), lambda at: (0, jnp.maximum(at - half, 0))),
            pl.BlockSpec((64, 128), lambda at: (0, 0)),
        ],
        compiler_params=PARAMS,
    )(acts, *larges, gain_part)


def pack_kernel(acts, sums, other, out):
    out[:ROWS, :] = acts[...]
    high, low = two_parts(sums[...] + other[...])
    for side in range(2):
        rows = slice(32 * side, 32 * side + 32)
        out[ROWS:, 128 * side : 128 * side + 128] = high[rows]
        out[ROWS:, 256 + 128 * side : 384 + 128 * side] = low[rows]
    out[ROWS:, 512:] = jnp.zeros((32, 256), BF16)


def pack(acts, sums, other):
    return pl.pallas_call(
        pack_kernel,
        out_shape=shape(ROWS + 32, acts.shape[1]),
        in_specs=[VMEM] * 3,
        out_specs=VMEM,
        compiler_params=PARAMS,
    )(acts, sums, other)


def relay_kernel(opposite, left, right, packed, packed_far, out, rounded):
    half = D // 2
    rows = slice(64, 128)
    out[:, :half] = (opposite[:, :half].astype(F32) + left[rows, :].astype(F32)).astype(BF16)
    out[:, half:D] = (opposite[:, half:].astype(F32) + right[rows, :].astype(F32)).astype(BF16)
    for side in range(2):
        here = slice(128 * side, 128 * side + 128)
        beside = slice(256 + 128 * side, 384 + 128 * side)
        mine, theirs = (
            ref[ROWS:, here].astype(F32) + ref[ROWS:, beside].astype(F32)
            for ref in (packed, packed_far)
        )
        high, low = two_parts(mine + theirs)
        rows = slice(32 * side, 32 * side + 32)
        out[rows, D : D + 128] = high
        out[rows, D + 128 :] = low
        rounded[rows, :] = high.astype(F32) + low.astype(F32)


def relay(opposite, left, right, packed, packed_far):
    return pl.pallas_call(
        relay_kernel,
        out_shape=[shape(64, D + 256), shape(64, 128, dtype=F32)],
        in_specs=[VMEM] * 5,
        out_specs=[VMEM] * 2,
        compiler_params=PARAMS,
    )(opposite, left, right, packed, packed_far)


FAR_WIDE = D + 8 * 128
LAST_WIDE = D + 16 * 128


def spread_kernel(kept, left, right, got, sums, near, far, *outs):
    half = D // 2
    other = got[:, D : D + 128].astype(F32) + got[:, D + 128 :].astype(F32)
    high, low = two_parts((sums[...] + near[...]) + (other + far[...]))
    for at in range(4):
        rows = slice(16 * at, 16 * at + 16)
        first = kept[rows, :half].astype(F32) + left[rows, :].astype(F32)
        outs[at][:, :half] = (first + got[rows, :half].astype(F32)).astype(BF16)
        first = kept[rows, half:].astype(F32) + right[rows, :].astype(F32)
        outs[at][:, half:D] = (first + got[rows, half:D].astype(F32)).astype(BF16)
        for k in range(4):
            left_edge = D + 128 * k
            outs[at][:, left_edge : left_edge + 128] = high[16 * k : 16 * k + 16]
            outs[at][:, left_edge + 512 : left_edge + 640] = low[16 * k : 16 * k + 16]


def spread(*parts):
    return pl.pallas_call(
        spread_kernel,
        out_shape=[shape(16, FAR_WIDE)] * 4,
        in_specs=[VMEM] * 7,
        out_specs=[VMEM] * 4,
        compiler_params=PARAMS,
    )(*parts)


def split_sum_kernel(place, *refs):
    for at in range(4):
        rows = slice(16 * at, 16 * at + 16)
        spot = pl.ds(pl.multiple_of(place[19 + at], 16), 16)
        refs[4][spot, :] = total([ref[rows, :] for ref in refs[:4]]).astype(BF16)


def split_sum(place, parts):
    return pl.pallas_call(
        split_sum_kernel,
        out_shape=shape(64, D),
        in_specs=[SMEM] + [VMEM] * 4,
        out_specs=VMEM,
        compiler_params=PARAMS,
    )(place, *parts)


def ends_kernel(*refs):
    mixed_ref, back_refs, outs = refs[0], refs[1:5], refs[5:]
    mixed = total([mixed_ref[16 * at : 16 * at + 16, :] for at in range(4)])
    back = total([ref[:, :D] for ref in back_refs])
    for at in range(4):
        rows = slice(4 * at, 4 * at + 4)
        outs[at][:, :D] = jnp.concatenate([mixed[rows], back[rows]], 0).astype(BF16)
    for k in range(4):
        here = slice(D + 128 * k, D + 128 * k + 128)
        beside = slice(D + 512 + 128 * k, D + 640 + 128 * k)
        block = total([ref[:, here].astype(F32) + ref[:, beside].astype(F32) for ref in back_refs])
        for side in range(2):
            high, low = two_parts(block[8 * side : 8 * side + 8])
            edge = D + 128 * (2 * k + side)
            for out in outs:
                out[:, edge : edge + 128] = high
                out[:, edge + 1024 : edge + 1152] = low


def ends(mixed, back_parts):
    return pl.pallas_call(
        ends_kernel,
        out_shape=[shape(8, LAST_WIDE)] * 4,
        in_specs=[VMEM] * 5,
        out_specs=[VMEM] * 4,
        compiler_params=PARAMS,
    )(mixed, *back_parts)


def finish_kernel(first, second, third, fourth, tokens, cotangent, gain, out, d_out, ln_out, qk_out):
    parts = (first, second, third, fourth)
    rows = total([ref[:, :D] for ref in parts])
    x_float = tokens[...].astype(F32)
    scaled, inv_std = standardize(x_float)
    out[...] = (x_float + rows[:4]).astype(BF16)
    d_norm = norm_back(rows[4:], scaled, inv_std, gain[...])
    d_out[...] = (cotangent[...].astype(F32) + d_norm).astype(BF16)
    for k in range(8):
        here = slice(D + 128 * k, D + 128 * k + 128)
        beside = slice(D + 1024 + 128 * k, D + 1152 + 128 * k)
        block = total([ref[:, here].astype(F32) + ref[:, beside].astype(F32) for ref in parts])
        if k < 6:
            for row in range(8):
                edge = 128 * (8 * k + row)
                ln_out[:, edge : edge + 128] = block[row : row + 1]
        if k == 6:
            qk_out[...] = block[:2]


def finish(parts, tokens, cotangent, gain):
    return pl.pallas_call(
        finish_kernel,
        out_shape=[
            shape(4, D),
            shape(4, D),
            shape(1, D, dtype=F32),
            shape(2, HD, dtype=F32),
        ],
        in_specs=[VMEM] * 7,
        out_specs=[VMEM] * 4,
        compiler_params=PARAMS,
    )(*parts, tokens, cotangent, gain)


def add_kernel(keep, taken, *outs):
    row = 0
    for out in outs:
        rows = slice(row, row + out.shape[0])
        out[...] = (keep[rows, :].astype(F32) + taken[rows, :].astype(F32)).astype(BF16)
        row += out.shape[0]


def add(keep, taken, heights):
    width = QUARTER // 2
    return pl.pallas_call(
        add_kernel,
        grid=(2,),
        out_shape=[shape(height, QUARTER) for height in heights],
        in_specs=[pl.BlockSpec((keep.shape[0], width), lambda at: (0, at))] * 2,
        out_specs=[pl.BlockSpec((height, width), lambda at: (0, at)) for height in heights],
    )(keep, taken)


def grads_kernel(place, acts, acts_far, n_ref, c_ref, far, *refs):
    keep, give, n_all, c_all, kept, given, sems, out_sems = refs
    half = D // 2
    own = pl.ds(pl.multiple_of(place[0] * half, half), half)
    top = pl.ds(0, ROWS)
    moves = [(n_ref.at[:, own], n_all.at[top]), (c_ref.at[:, own], c_all.at[top])]
    for at in range(16):
        row = pl.multiple_of(place[3 + at], 32)
        spot = pl.ds(ROWS + 16 * at, 16)
        moves.append((far.at[pl.ds(row, 16)], n_all.at[spot]))
        moves.append((far.at[pl.ds(row + 16, 16)], c_all.at[spot]))
    loads = []
    for at, (source, target) in enumerate(moves):
        copy = pltpu.make_async_copy(source, target, sems.at[at])
        copy.start()
        loads.append(copy)
    whole = jnp.concatenate([acts[:ROWS, :], acts_far[:ROWS, :]], 0)
    ins, heads = 3 * HD // 2, 2 * HD
    units = (whole.shape[1] - heads) // 2
    for copy in loads:
        copy.wait()
    stores = []
    for at, (buffer, target, column) in enumerate(
        ((given, give, 1 - place[1]), (kept, keep, place[1]))
    ):
        span = pl.ds(pl.multiple_of(column * QUARTER, QUARTER), QUARTER)
        row = 0
        for left, right in (
            (whole[:, :ins], n_all),
            (whole[:, heads : heads + units], n_all),
            (whole[:, ins:heads], c_all),
            (whole[:, heads + units :], c_all),
        ):
            height = left.shape[1]
            buffer[row : row + height, :] = row_contract(left, right[:, span]).astype(BF16)
            row += height
        copy = pltpu.make_async_copy(buffer, target, out_sems.at[at])
        copy.start()
        stores.append(copy)
    for copy in stores:
        copy.wait()


def grads(place, acts, acts_far, n_all, c_all, far):
    height = acts.shape[1]
    return pl.pallas_call(
        grads_kernel,
        out_shape=[shape(height, QUARTER)] * 2,
        in_specs=[SMEM] + [VMEM] * 2 + [ANY] * 3,
        out_specs=[ANY] * 2,
        scratch_shapes=[
            pltpu.VMEM((2 * ROWS, D // 2), BF16),
            pltpu.VMEM((2 * ROWS, D // 2), BF16),
            pltpu.VMEM((height, QUARTER), BF16),
            pltpu.VMEM((height, QUARTER), BF16),
            pltpu.SemaphoreType.DMA((34,)),
            pltpu.SemaphoreType.DMA((2,)),
        ],
        compiler_params=PARAMS,
    )(place, acts, acts_far, n_all, c_all, far)


def all_to_all(block, unit):
    groups = [
        [first + unit * at for at in range(4)]
        for first in range(64)
        if first // unit % 4 == 0
    ]
    return lax.all_to_all(block, "mp", 0, 0, axis_index_groups=groups, tiled=True)


def all_planes(block):
    planes = [[Y * up + Z * deep + X * at for up in range(4) for at in range(4)] for deep in range(4)]
    return lax.all_gather(block, "mp", axis=0, tiled=True, axis_index_groups=planes)


def local(tokens, cotangent, ln_gain, qk_gain, w_qkv, w_mlp_in, w_attn_out, w_mlp_out):
    tie = lax.optimization_barrier
    dp, mp = lax.axis_index("dp"), lax.axis_index("mp")
    up, at = mp // Y, mp % 4
    starts = [32 * (4 * (up ^ high) + (at ^ low)) for high in range(4) for low in range(4)]
    starts += [16 * (at ^ step) for step in range(4)] + [16 * (up ^ step) for step in range(4)]
    place = jnp.stack([dp // 2, dp % 2, mp % 2] + starts).astype(jnp.int32)
    cols, units = w_qkv.shape[1], w_mlp_in.shape[0]
    offset = mp % 2 * cols
    gains = jnp.concatenate(
        [
            lax.dynamic_slice_in_dim(qk_gain, offset, cols, 1),
            lax.dynamic_slice_in_dim(qk_gain, cols - offset, cols, 1),
        ],
        1,
    )
    gain_row = ln_gain.reshape(1, D)
    w_flat = w_qkv.reshape(3 * cols, D)

    n_rows, c_rows, away = apart(place, tie(pieces(start(tokens, cotangent, gain_row), Z)))
    n_parts, c_rows = tie((pieces(n_rows, X), all_to_all(c_rows, Y)))
    n_rows = join(n_parts)
    n_rows, c_rows, away = tie((n_rows, c_rows, away))
    n_parts, c_parts, there = tie((pieces(n_rows, Y), two_steps(c_rows), swapped(away, "dp", 2)))
    far = all_planes(there)
    n_all, c_all, qk_own, own = first(place, n_parts, c_parts, w_flat, w_attn_out)

    peer = swapped(own, "mp", X)
    ad = hidden(n_all, c_all, w_mlp_in, w_mlp_out)
    peer, ad = tie((peer, ad))
    acts, gain_part = head(place, qk_own, own, peer, gains, ad)
    outs = back(acts, w_attn_out, w_mlp_out, w_flat, w_mlp_in, n_all, gain_row, gain_part)
    kept, opposite, left, right, sums = outs[4:]
    left, right = swapped(left, "mp", X), swapped(right, "mp", 3 * X)
    near, late = swapped(outs[1], "mp", Y), swapped(outs[3], "mp", 3 * Y)
    packed = pack(acts, sums, swapped(sums, "dp", 1))
    packed_far = swapped(packed, "dp", 2)
    left, right, near, late, packed_far = tie((left, right, near, late, packed_far))
    relayed, sums = relay(opposite, left, right, packed, packed_far)
    relayed, middle, packed_far = tie((relayed, outs[2], packed_far))
    got, middle = swapped(relayed, "mp", 2 * X), swapped(middle, "mp", 2 * Y)
    other_sums = swapped(sums, "mp", X), swapped(sums, "mp", 3 * X)
    keep, give = grads(place, packed, packed_far, n_all, c_all, far)
    got, middle, other_sums, keep, give = tie((got, middle, other_sums, keep, give))
    taken = swapped(give, "dp", 1)
    spreads = spread(kept, left, right, got, sums, *other_sums)
    spreads, middle = tie((spreads, middle))
    back_parts = exchanged(spreads, Y)
    mixed = all_to_all(split_sum(place, [outs[0], near, middle, late]), X)
    last = exchanged(ends(mixed, back_parts), Z)
    parts = add(keep, taken, (3 * cols, units, cols, units))
    last, parts = tie((last, parts))
    output, d_tokens, g_ln, g_qk = finish(last, tokens, cotangent, gain_row)
    return (
        output,
        d_tokens,
        g_ln.reshape(D),
        g_qk,
        parts[0].reshape(3, cols, QUARTER),
        *parts[1:],
    )


def solution(mesh):
    return jax.shard_map(
        local,
        mesh=mesh,
        in_specs=(
            P(("dp", "mp"), None),
            P(("dp", "mp"), None),
            P(),
            P(),
            P(None, "mp", None),
            P("mp", None),
            P("mp", None),
            P("mp", None),
        ),
        out_specs=(
            P(("dp", "mp"), None),
            P(("dp", "mp"), None),
            P(),
            P(),
            P(None, "mp", "dp"),
            P("mp", "dp"),
            P("mp", "dp"),
            P("mp", "dp"),
        ),
        check_vma=False,
    )
```

```python
import functools
import math

import jax
import jax.numpy as jnp
from jax import lax
from jax.experimental import pallas as pl
from jax.experimental.pallas import tpu as pltpu
from jax.sharding import PartitionSpec as P

D = 6144
HD = 128
ROWS = 256
QUARTER = D // 4
EPS = 1e-06
X, Z, Y = 1, 4, 16
BF16 = jnp.bfloat16
F32 = jnp.float32
VMEM = pl.BlockSpec(memory_space=pltpu.VMEM)
SMEM = pl.BlockSpec(memory_space=pltpu.SMEM)
ANY = pl.BlockSpec(memory_space=pl.ANY)
PARAMS = pltpu.CompilerParams(vmem_limit_bytes=48 * 1024 * 1024)


def shape(*dims, dtype=BF16):
    return jax.ShapeDtypeStruct(dims, dtype)


def swapped(block, axis, mask):
    count = lax.axis_size(axis)
    return lax.ppermute(block, axis, [(low, low ^ mask) for low in range(count)])


def pieces(block, unit):
    return [block] + [swapped(block, "mp", step * unit) for step in (1, 2, 3)]


def exchanged(blocks, unit):
    return [blocks[0]] + [swapped(blocks[step], "mp", step * unit) for step in (1, 2, 3)]


def two_steps(block):
    half = block.shape[1] // 2
    opposite = swapped(block, "mp", 2 * X)
    pair = jnp.concatenate([block, opposite], 0)
    return [
        block,
        opposite,
        swapped(pair[:, :half], "mp", X),
        swapped(pair[:, half:], "mp", 3 * X),
    ]


def total(blocks):
    first, second, third, fourth = (block.astype(F32) for block in blocks)
    return (first + second) + (third + fourth)


def two_parts(values):
    high = values.astype(BF16)
    return high, (values - high.astype(F32)).astype(BF16)


def standardize(values):
    average = jnp.mean(values, -1, keepdims=True)
    centered = values - average
    inv_std = lax.rsqrt(jnp.mean(centered * centered, -1, keepdims=True) + EPS)
    return (centered * inv_std, inv_std)


def norm_back(gradient, scaled, inv_std, gain_row):
    weighted = gradient * gain_row
    return inv_std * (
        weighted
        - jnp.mean(weighted, -1, keepdims=True)
        - scaled * jnp.mean(weighted * scaled, -1, keepdims=True)
    )


def times_rows(left, weight):
    return lax.dot_general(left, weight, (((1,), (1,)), ((), ())), preferred_element_type=F32)


def row_contract(left, right):
    return lax.dot_general(left, right, (((0,), (0,)), ((), ())), preferred_element_type=F32)


def dot(left, right):
    return jnp.dot(left, right, preferred_element_type=F32)


def start_kernel(tokens, cotangent, gain, out):
    scaled, _ = standardize(tokens[...].astype(F32))
    both = jnp.concatenate([scaled * gain[...], cotangent[...].astype(F32)], 0)
    out[...] = both.astype(BF16)


def start(tokens, cotangent, gain):
    return pl.pallas_call(
        start_kernel,
        grid=(1,),
        out_shape=shape(8, D),
        in_specs=[pl.BlockSpec((rows, D), lambda at: (0, 0)) for rows in (4, 4, 1)],
        out_specs=pl.BlockSpec((8, D), lambda at: (0, 0)),
        compiler_params=PARAMS,
    )(tokens, cotangent, gain)


def apart_kernel(place, *refs):
    n_out, c_out, away = refs[4:]
    left = pl.multiple_of((1 - place[0]) * (D // 2), D // 2)
    for part, (out, rows) in enumerate(((n_out, slice(0, 16)), (c_out, slice(16, 32)))):
        half = slice(4 * part, 4 * part + 4)
        blocks = [ref[...].astype(F32)[half] for ref in refs[:4]]
        whole = jnp.concatenate(blocks, 0).astype(BF16)
        for at in range(out.shape[0] // 16):
            out[16 * at : 16 * at + 16, :] = whole
        away[rows, :] = out[0:16, pl.ds(left, D // 2)]


def apart(place, parts):
    return pl.pallas_call(
        apart_kernel,
        out_shape=[shape(16, D), shape(64, D), shape(32, D // 2)],
        in_specs=[SMEM] + [VMEM] * 4,
        out_specs=[VMEM] * 3,
        compiler_params=PARAMS,
    )(place, *parts)


def join_kernel(*refs):
    for at in range(4):
        refs[4][16 * at : 16 * at + 16, :] = refs[at][...]


def join(parts):
    return pl.pallas_call(
        join_kernel,
        out_shape=shape(64, D),
        in_specs=[VMEM] * 4,
        out_specs=VMEM,
        compiler_params=PARAMS,
    )(*parts)


def n_moves(parts, target):
    return [(parts[at], target.at[pl.ds(64 * at, 64)]) for at in range(4)]


def c_moves(place, parts, target):
    half = parts[0].shape[1] // 2
    left, right = pl.ds(0, half), pl.ds(half, half)
    moves = []
    for up in range(4):
        first = pl.multiple_of(place[23 + up], 16)
        rows, lower = pl.ds(first, 16), pl.ds(64 + first, 16)
        spots = [pl.ds(64 * up + 16 * at, 16) for at in range(4)]
        moves += [
            (parts[0].at[rows], target.at[spots[0]]),
            (parts[1].at[rows], target.at[spots[2]]),
            (parts[2].at[rows], target.at[spots[1], left]),
            (parts[2].at[lower], target.at[spots[3], left]),
            (parts[3].at[rows], target.at[spots[3], right]),
            (parts[3].at[lower], target.at[spots[1], right]),
        ]
    return moves


def first_kernel(*refs):
    place, n_parts, c_parts, weights = refs[0], refs[1:5], refs[5:9], refs[9:11]
    n_out, c_out, qk_ref, send_ref = refs[11:15]
    n_all, c_all, wq, wo, sems = refs[15:]
    copies = []

    def begin(source, target):
        copy = pltpu.make_async_copy(source, target, sems.at[len(copies)])
        copy.start()
        copies.append(copy)
        return copy

    n_in = [begin(*move) for move in n_moves(n_parts, n_all)]
    wq_in = begin(weights[0], wq)
    c_in = [begin(*move) for move in c_moves(place, c_parts, c_all)]
    wo_in = begin(weights[1], wo)
    for copy in n_in:
        copy.wait()
    wq_in.wait()
    n_done = begin(n_all, n_out)
    cols = wo.shape[0]
    projected = jnp.zeros((ROWS, 3 * cols), F32)
    for at in range(4):
        span = slice(QUARTER * at, QUARTER * at + QUARTER)
        projected += times_rows(n_all[:, span], wq[:, span])
    queries = projected[:, : 2 * cols]
    qk_ref[...] = queries
    send_ref[:, : 2 * cols], send_ref[:, 2 * cols : 4 * cols] = two_parts(queries)
    for copy in c_in:
        copy.wait()
    wo_in.wait()
    c_done = begin(c_all, c_out)
    d_context = jnp.zeros((ROWS, cols), F32)
    for at in range(4):
        span = slice(QUARTER * at, QUARTER * at + QUARTER)
        d_context += times_rows(c_all[:, span], wo[:, span])
    values = projected[:, 2 * cols :]
    send_ref[:, 4 * cols :] = jnp.concatenate([values, d_context], 1).astype(BF16)
    n_done.wait()
    c_done.wait()


def first(place, n_parts, c_parts, w_flat, w_out):
    cols = w_out.shape[0]
    return pl.pallas_call(
        first_kernel,
        out_shape=[
            shape(ROWS, D),
            shape(ROWS, D),
            shape(ROWS, 2 * cols, dtype=F32),
            shape(ROWS, 6 * cols),
        ],
        in_specs=[SMEM] + [ANY] * 10,
        out_specs=[ANY, ANY, VMEM, VMEM],
        scratch_shapes=[
            pltpu.VMEM((ROWS, D), BF16),
            pltpu.VMEM((ROWS, D), BF16),
            pltpu.VMEM((3 * cols, D), BF16),
            pltpu.VMEM((cols, D), BF16),
            pltpu.SemaphoreType.DMA((32,)),
        ],
        compiler_params=PARAMS,
    )(place, *n_parts, *c_parts, w_flat, w_out)


def hidden_kernel(n_ref, c_ref, win, wout, out, *scratch):
    n_all, c_all, w_in, w_out, sems = scratch
    loads = []
    for at in range(4):
        span = pl.ds(QUARTER * at, QUARTER)
        pairs = ((n_ref, n_all), (win, w_in), (c_ref, c_all), (wout, w_out))
        for which, (source, target) in enumerate(pairs):
            copy = pltpu.make_async_copy(
                source.at[:, span], target.at[:, span], sems.at[at, which]
            )
            copy.start()
            loads.append(copy)
    units = w_in.shape[0]
    hidden = jnp.zeros((ROWS, units), F32)
    d_act = jnp.zeros((ROWS, units), F32)
    for at in range(4):
        for copy in loads[4 * at : 4 * at + 4]:
            copy.wait()
        span = slice(QUARTER * at, QUARTER * at + QUARTER)
        hidden += times_rows(n_all[:, span], w_in[:, span])
        d_act += times_rows(c_all[:, span], w_out[:, span])
    cdf = 0.5 * (1.0 + lax.erf(hidden * 0.7071067811865476))
    pdf = jnp.exp(-0.5 * hidden * hidden) * 0.3989422804014327
    out[:, units:] = (hidden * cdf).astype(BF16)
    out[:, :units] = (d_act.astype(BF16).astype(F32) * (cdf + hidden * pdf)).astype(BF16)


def hidden(n_all, c_all, w_in, w_out):
    units = w_in.shape[0]
    return pl.pallas_call(
        hidden_kernel,
        out_shape=shape(ROWS, 2 * units),
        in_specs=[ANY] * 4,
        out_specs=VMEM,
        scratch_shapes=[
            pltpu.VMEM((ROWS, D), BF16),
            pltpu.VMEM((ROWS, D), BF16),
            pltpu.VMEM((units, D), BF16),
            pltpu.VMEM((units, D), BF16),
            pltpu.SemaphoreType.DMA((4, 4)),
        ],
        compiler_params=PARAMS,
    )(n_all, c_all, w_in, w_out)


def head_kernel(place, qk_own, own, peer, gains, ad, out, gain_ref):
    cols = HD // 2
    other = jnp.concatenate(
        [peer[16 * (at ^ 1) : 16 * (at ^ 1) + 16, :] for at in range(ROWS // 16)], 0
    )
    qk_other = other[:, :HD].astype(F32) + other[:, HD : 2 * HD].astype(F32)
    query = jnp.concatenate([qk_own[:, :cols], qk_other[:, :cols]], 1)
    key = jnp.concatenate([qk_own[:, cols:], qk_other[:, cols:]], 1)
    left, right = slice(2 * HD, 2 * HD + cols), slice(2 * HD + cols, 3 * HD)
    values = jnp.concatenate([own[:, left], other[:, left]], 1)
    d_ctx = jnp.concatenate([own[:, right], other[:, right]], 1)
    q_gain, k_gain = gains[0:1, :], gains[1:2, :]
    q_scaled, q_inv = standardize(query)
    k_scaled, k_inv = standardize(key)
    q_normed = (q_scaled * q_gain).astype(BF16)
    k_normed = (k_scaled * k_gain).astype(BF16)
    scores = times_rows(q_normed, k_normed) * (1.0 / math.sqrt(HD))
    grown = jnp.exp(scores - jnp.max(scores, -1, keepdims=True))
    probs = (grown / jnp.sum(grown, -1, keepdims=True)).astype(BF16)
    context = dot(probs, values)[:, :cols]
    d_probs = times_rows(d_ctx, values)
    probs_f = probs.astype(F32)
    centered = d_probs - jnp.sum(probs_f * d_probs, -1, keepdims=True)
    d_scores = (probs_f * centered * (1.0 / math.sqrt(HD))).astype(BF16)
    d_values = row_contract(probs, d_ctx)
    d_qn = dot(d_scores, k_normed)
    d_kn = row_contract(d_scores, q_normed)
    d_query = norm_back(d_qn, q_scaled, q_inv, q_gain)
    d_key = norm_back(d_kn, k_scaled, k_inv, k_gain)
    out[:, :HD] = jnp.concatenate([d_query[:, :cols], d_key[:, :cols]], 1).astype(BF16)
    out[:, HD : 2 * HD] = jnp.concatenate([d_values[:, :cols], context], 1).astype(BF16)
    out[:, 2 * HD :] = ad[...]
    for row, terms in enumerate((d_qn * q_scaled, d_kn * k_scaled)):
        mine = jnp.sum(terms, 0, keepdims=True)[:, :cols]
        none = jnp.zeros_like(mine)
        even = jnp.concatenate([mine, none], 1)
        odd = jnp.concatenate([none, mine], 1)
        gain_ref[row : row + 1, :] = jnp.where(place[2] == 0, even, odd)


def head(place, qk_own, own, peer, gains, ad):
    return pl.pallas_call(
        head_kernel,
        out_shape=[shape(ROWS, 2 * HD + ad.shape[1]), shape(2, HD, dtype=F32)],
        in_specs=[SMEM] + [VMEM] * 5,
        out_specs=[VMEM] * 2,
        compiler_params=PARAMS,
    )(place, qk_own, own, peer, gains, ad)


SLAB = 1536
STEPS = D // SLAB


def back_kernel(acts, w_ao, w_mo, w_qkv, w_mi, n_ref, gain, gain_part, *outs):
    mix_outs, kept, opposite, near_left, near_right, sums = outs[:4], *outs[4:]
    at = pl.program_id(0)
    ins, units, heads = w_qkv.shape[0], w_mi.shape[0], 2 * HD
    d_norm = dot(acts[:, :ins], w_qkv[...]) + dot(acts[:, heads : heads + units], w_mi[...])
    part = jnp.sum(d_norm * n_ref[...].astype(F32), 0, keepdims=True) / gain[...]

    @pl.when(at == 0)
    def _():
        sums[48:64, :] = jnp.zeros((16, 128), F32)
        sums[48:50, :] = gain_part[...]

    for k in range(SLAB // 128):
        sums[pl.ds(SLAB // 128 * at + k, 1), :] = part[:, 128 * k : 128 * k + 128]

    chunks = [
        jnp.concatenate(
            [d_norm[64 * up + 16 * k : 64 * up + 16 * k + 16] for up in range(4)], 0
        ).astype(BF16)
        for k in range(4)
    ]
    kept[...] = chunks[0]
    opposite[...] = chunks[2]

    @pl.when(at < STEPS // 2)
    def _():
        near_left[:64, :] = chunks[1]
        near_left[64:, :] = chunks[3]

    @pl.when(at >= STEPS // 2)
    def _():
        near_right[:64, :] = chunks[3]
        near_right[64:, :] = chunks[1]

    mixed = dot(acts[:, ins:heads], w_ao[...]) + dot(acts[:, heads + units :], w_mo[...])
    for k in range(4):
        mix_outs[k][...] = mixed[64 * k : 64 * k + 64].astype(BF16)


def back(acts, w_ao, w_mo, w_qkv, w_mi, n_all, ln_gain, gain_part):
    larges = (w_ao, w_mo, w_qkv, w_mi, n_all, ln_gain)
    half = STEPS // 2
    return pl.pallas_call(
        back_kernel,
        grid=(STEPS,),
        out_shape=[shape(64, D)] * 6
        + [shape(128, D // 2)] * 2
        + [shape(64, 128, dtype=F32)],
        in_specs=[pl.BlockSpec(acts.shape, lambda at: (0, 0))]
        + [pl.BlockSpec((one.shape[0], SLAB), lambda at: (0, at)) for one in larges]
        + [pl.BlockSpec(gain_part.shape, lambda at: (0, 0))],
        out_specs=[pl.BlockSpec((64, SLAB), lambda at: (0, at))] * 6
        + [
            pl.BlockSpec((128, SLAB), lambda at: (0, jnp.minimum(at, half - 1))),
            pl.BlockSpec((128, SLAB), lambda at: (0, jnp.maximum(at - half, 0))),
            pl.BlockSpec((64, 128), lambda at: (0, 0)),
        ],
        compiler_params=PARAMS,
    )(acts, *larges, gain_part)


def pack_kernel(acts, sums, other, out):
    out[:ROWS, :] = acts[...]
    high, low = two_parts(sums[...] + other[...])
    for side in range(2):
        rows = slice(32 * side, 32 * side + 32)
        out[ROWS:, 128 * side : 128 * side + 128] = high[rows]
        out[ROWS:, 256 + 128 * side : 384 + 128 * side] = low[rows]
    out[ROWS:, 512:] = jnp.zeros((32, 256), BF16)


def pack(acts, sums, other):
    return pl.pallas_call(
        pack_kernel,
        out_shape=shape(ROWS + 32, acts.shape[1]),
        in_specs=[VMEM] * 3,
        out_specs=VMEM,
        compiler_params=PARAMS,
    )(acts, sums, other)


def relay_kernel(opposite, left, right, packed, packed_far, out, rounded):
    half = D // 2
    rows = slice(64, 128)
    out[:, :half] = (opposite[:, :half].astype(F32) + left[rows, :].astype(F32)).astype(BF16)
    out[:, half:D] = (opposite[:, half:].astype(F32) + right[rows, :].astype(F32)).astype(BF16)
    for side in range(2):
        here = slice(128 * side, 128 * side + 128)
        beside = slice(256 + 128 * side, 384 + 128 * side)
        mine, theirs = (
            ref[ROWS:, here].astype(F32) + ref[ROWS:, beside].astype(F32)
            for ref in (packed, packed_far)
        )
        high, low = two_parts(mine + theirs)
        rows = slice(32 * side, 32 * side + 32)
        out[rows, D : D + 128] = high
        out[rows, D + 128 :] = low
        rounded[rows, :] = high.astype(F32) + low.astype(F32)


def relay(opposite, left, right, packed, packed_far):
    return pl.pallas_call(
        relay_kernel,
        out_shape=[shape(64, D + 256), shape(64, 128, dtype=F32)],
        in_specs=[VMEM] * 5,
        out_specs=[VMEM] * 2,
        compiler_params=PARAMS,
    )(opposite, left, right, packed, packed_far)


FAR_WIDE = D + 8 * 128
LAST_WIDE = D + 16 * 128


def spread_kernel(kept, left, right, got, sums, near, far, *outs):
    half = D // 2
    other = got[:, D : D + 128].astype(F32) + got[:, D + 128 :].astype(F32)
    high, low = two_parts((sums[...] + near[...]) + (other + far[...]))
    for at in range(4):
        rows = slice(16 * at, 16 * at + 16)
        first = kept[rows, :half].astype(F32) + left[rows, :].astype(F32)
        outs[at][:, :half] = (first + got[rows, :half].astype(F32)).astype(BF16)
        first = kept[rows, half:].astype(F32) + right[rows, :].astype(F32)
        outs[at][:, half:D] = (first + got[rows, half:D].astype(F32)).astype(BF16)
        for k in range(4):
            left_edge = D + 128 * k
            outs[at][:, left_edge : left_edge + 128] = high[16 * k : 16 * k + 16]
            outs[at][:, left_edge + 512 : left_edge + 640] = low[16 * k : 16 * k + 16]


def spread(*parts):
    return pl.pallas_call(
        spread_kernel,
        out_shape=[shape(16, FAR_WIDE)] * 4,
        in_specs=[VMEM] * 7,
        out_specs=[VMEM] * 4,
        compiler_params=PARAMS,
    )(*parts)


def split_sum_kernel(*refs):
    for at in range(4):
        rows = slice(16 * at, 16 * at + 16)
        refs[4 + at][...] = total([ref[rows, :] for ref in refs[:4]]).astype(BF16)


def split_sum(parts):
    return pl.pallas_call(
        split_sum_kernel,
        out_shape=[shape(16, D)] * 4,
        in_specs=[VMEM] * 4,
        out_specs=[VMEM] * 4,
        compiler_params=PARAMS,
    )(*parts)


def ends_kernel(*refs):
    mixed_refs, back_refs, outs = refs[:4], refs[4:8], refs[8:]
    mixed = total([ref[...] for ref in mixed_refs])
    back = total([ref[:, :D] for ref in back_refs])
    for at in range(4):
        rows = slice(4 * at, 4 * at + 4)
        outs[at][:, :D] = jnp.concatenate([mixed[rows], back[rows]], 0).astype(BF16)
    for k in range(4):
        here = slice(D + 128 * k, D + 128 * k + 128)
        beside = slice(D + 512 + 128 * k, D + 640 + 128 * k)
        block = total([ref[:, here].astype(F32) + ref[:, beside].astype(F32) for ref in back_refs])
        for side in range(2):
            high, low = two_parts(block[8 * side : 8 * side + 8])
            edge = D + 128 * (2 * k + side)
            for out in outs:
                out[:, edge : edge + 128] = high
                out[:, edge + 1024 : edge + 1152] = low


def ends(mixed_parts, back_parts):
    return pl.pallas_call(
        ends_kernel,
        out_shape=[shape(8, LAST_WIDE)] * 4,
        in_specs=[VMEM] * 8,
        out_specs=[VMEM] * 4,
        compiler_params=PARAMS,
    )(*mixed_parts, *back_parts)


def finish_kernel(first, second, third, fourth, tokens, cotangent, gain, out, d_out, ln_out, qk_out):
    parts = (first, second, third, fourth)
    rows = total([ref[:, :D] for ref in parts])
    x_float = tokens[...].astype(F32)
    scaled, inv_std = standardize(x_float)
    out[...] = (x_float + rows[:4]).astype(BF16)
    d_norm = norm_back(rows[4:], scaled, inv_std, gain[...])
    d_out[...] = (cotangent[...].astype(F32) + d_norm).astype(BF16)
    for k in range(8):
        here = slice(D + 128 * k, D + 128 * k + 128)
        beside = slice(D + 1024 + 128 * k, D + 1152 + 128 * k)
        block = total([ref[:, here].astype(F32) + ref[:, beside].astype(F32) for ref in parts])
        if k < 6:
            for row in range(8):
                edge = 128 * (8 * k + row)
                ln_out[:, edge : edge + 128] = block[row : row + 1]
        if k == 6:
            qk_out[...] = block[:2]


def finish(parts, tokens, cotangent, gain):
    return pl.pallas_call(
        finish_kernel,
        out_shape=[
            shape(4, D),
            shape(4, D),
            shape(1, D, dtype=F32),
            shape(2, HD, dtype=F32),
        ],
        in_specs=[VMEM] * 7,
        out_specs=[VMEM] * 4,
        compiler_params=PARAMS,
    )(*parts, tokens, cotangent, gain)


def add_kernel(keep, taken, *outs):
    row = 0
    for out in outs:
        rows = slice(row, row + out.shape[0])
        out[...] = (keep[rows, :].astype(F32) + taken[rows, :].astype(F32)).astype(BF16)
        row += out.shape[0]


def add(keep, taken, heights):
    width = QUARTER // 2
    return pl.pallas_call(
        add_kernel,
        grid=(2,),
        out_shape=[shape(height, QUARTER) for height in heights],
        in_specs=[pl.BlockSpec((keep.shape[0], width), lambda at: (0, at))] * 2,
        out_specs=[pl.BlockSpec((height, width), lambda at: (0, at)) for height in heights],
    )(keep, taken)


def grads_kernel(place, acts, acts_far, n_ref, c_ref, far, *refs):
    keep, give, n_all, c_all, kept, given, sems, out_sems = refs
    half = D // 2
    own = pl.ds(pl.multiple_of(place[0] * half, half), half)
    top = pl.ds(0, ROWS)
    moves = [(n_ref.at[:, own], n_all.at[top]), (c_ref.at[:, own], c_all.at[top])]
    for at in range(16):
        row = pl.multiple_of(place[3 + at], 32)
        spot = pl.ds(ROWS + 16 * at, 16)
        moves.append((far.at[pl.ds(row, 16)], n_all.at[spot]))
        moves.append((far.at[pl.ds(row + 16, 16)], c_all.at[spot]))
    loads = []
    for at, (source, target) in enumerate(moves):
        copy = pltpu.make_async_copy(source, target, sems.at[at])
        copy.start()
        loads.append(copy)
    whole = jnp.concatenate([acts[:ROWS, :], acts_far[:ROWS, :]], 0)
    ins, heads = 3 * HD // 2, 2 * HD
    units = (whole.shape[1] - heads) // 2
    for copy in loads:
        copy.wait()
    stores = []
    for at, (buffer, target, column) in enumerate(
        ((given, give, 1 - place[1]), (kept, keep, place[1]))
    ):
        span = pl.ds(pl.multiple_of(column * QUARTER, QUARTER), QUARTER)
        row = 0
        for left, right in (
            (whole[:, :ins], n_all),
            (whole[:, heads : heads + units], n_all),
            (whole[:, ins:heads], c_all),
            (whole[:, heads + units :], c_all),
        ):
            height = left.shape[1]
            buffer[row : row + height, :] = row_contract(left, right[:, span]).astype(BF16)
            row += height
        copy = pltpu.make_async_copy(buffer, target, out_sems.at[at])
        copy.start()
        stores.append(copy)
    for copy in stores:
        copy.wait()


def grads(place, acts, acts_far, n_all, c_all, far):
    height = acts.shape[1]
    return pl.pallas_call(
        grads_kernel,
        out_shape=[shape(height, QUARTER)] * 2,
        in_specs=[SMEM] + [VMEM] * 2 + [ANY] * 3,
        out_specs=[ANY] * 2,
        scratch_shapes=[
            pltpu.VMEM((2 * ROWS, D // 2), BF16),
            pltpu.VMEM((2 * ROWS, D // 2), BF16),
            pltpu.VMEM((height, QUARTER), BF16),
            pltpu.VMEM((height, QUARTER), BF16),
            pltpu.SemaphoreType.DMA((34,)),
            pltpu.SemaphoreType.DMA((2,)),
        ],
        compiler_params=PARAMS,
    )(place, acts, acts_far, n_all, c_all, far)


def all_to_all(block, unit):
    groups = [
        [first + unit * at for at in range(4)]
        for first in range(64)
        if first // unit % 4 == 0
    ]
    return lax.all_to_all(block, "mp", 0, 0, axis_index_groups=groups, tiled=True)


def all_planes(block):
    planes = [[Y * up + Z * deep + X * at for up in range(4) for at in range(4)] for deep in range(4)]
    return lax.all_gather(block, "mp", axis=0, tiled=True, axis_index_groups=planes)


def local(tokens, cotangent, ln_gain, qk_gain, w_qkv, w_mlp_in, w_attn_out, w_mlp_out):
    tie = lax.optimization_barrier
    dp, mp = lax.axis_index("dp"), lax.axis_index("mp")
    up, at = mp // Y, mp % 4
    starts = [32 * (4 * (up ^ high) + (at ^ low)) for high in range(4) for low in range(4)]
    starts += [16 * (at ^ step) for step in range(4)] + [16 * (up ^ step) for step in range(4)]
    place = jnp.stack([dp // 2, dp % 2, mp % 2] + starts).astype(jnp.int32)
    cols, units = w_qkv.shape[1], w_mlp_in.shape[0]
    offset = mp % 2 * cols
    gains = jnp.concatenate(
        [
            lax.dynamic_slice_in_dim(qk_gain, offset, cols, 1),
            lax.dynamic_slice_in_dim(qk_gain, cols - offset, cols, 1),
        ],
        1,
    )
    gain_row = ln_gain.reshape(1, D)
    w_flat = w_qkv.reshape(3 * cols, D)

    n_rows, c_rows, away = apart(place, tie(pieces(start(tokens, cotangent, gain_row), Z)))
    n_parts, c_rows = tie((pieces(n_rows, X), all_to_all(c_rows, Y)))
    n_rows = join(n_parts)
    n_rows, c_rows, away = tie((n_rows, c_rows, away))
    n_parts, c_parts, there = tie((pieces(n_rows, Y), two_steps(c_rows), swapped(away, "dp", 2)))
    far = all_planes(there)
    n_all, c_all, qk_own, own = first(place, n_parts, c_parts, w_flat, w_attn_out)

    peer = swapped(own, "mp", X)
    ad = hidden(n_all, c_all, w_mlp_in, w_mlp_out)
    peer, ad = tie((peer, ad))
    acts, gain_part = head(place, qk_own, own, peer, gains, ad)
    outs = back(acts, w_attn_out, w_mlp_out, w_flat, w_mlp_in, n_all, gain_row, gain_part)
    kept, opposite, left, right, sums = outs[4:]
    left, right = swapped(left, "mp", X), swapped(right, "mp", 3 * X)
    near, late = swapped(outs[1], "mp", Y), swapped(outs[3], "mp", 3 * Y)
    packed = pack(acts, sums, swapped(sums, "dp", 1))
    packed_far = swapped(packed, "dp", 2)
    left, right, near, late, packed_far = tie((left, right, near, late, packed_far))
    relayed, sums = relay(opposite, left, right, packed, packed_far)
    relayed, middle, packed_far = tie((relayed, outs[2], packed_far))
    got, middle = swapped(relayed, "mp", 2 * X), swapped(middle, "mp", 2 * Y)
    other_sums = swapped(sums, "mp", X), swapped(sums, "mp", 3 * X)
    keep, give = grads(place, packed, packed_far, n_all, c_all, far)
    got, middle, other_sums, keep, give = tie((got, middle, other_sums, keep, give))
    taken = swapped(give, "dp", 1)
    spreads = spread(kept, left, right, got, sums, *other_sums)
    spreads, middle = tie((spreads, middle))
    back_parts = exchanged(spreads, Y)
    mixed = exchanged(split_sum([outs[0], near, middle, late]), X)
    last = exchanged(ends(mixed, back_parts), Z)
    parts = add(keep, taken, (3 * cols, units, cols, units))
    last, parts = tie((last, parts))
    output, d_tokens, g_ln, g_qk = finish(last, tokens, cotangent, gain_row)
    return (
        output,
        d_tokens,
        g_ln.reshape(D),
        g_qk,
        parts[0].reshape(3, cols, QUARTER),
        *parts[1:],
    )


def solution(mesh):
    return jax.shard_map(
        local,
        mesh=mesh,
        in_specs=(
            P(("dp", "mp"), None),
            P(("dp", "mp"), None),
            P(),
            P(),
            P(None, "mp", None),
            P("mp", None),
            P("mp", None),
            P("mp", None),
        ),
        out_specs=(
            P(("dp", "mp"), None),
            P(("dp", "mp"), None),
            P(),
            P(),
            P(None, "mp", "dp"),
            P("mp", "dp"),
            P("mp", "dp"),
            P("mp", "dp"),
        ),
        check_vma=False,
    )
```
